512 devices in a mesh: expert: 8 (over x, y_hi), etp: 64 (over z, y_lo, core).
Axes of the slice: x: 4, y: 4 (y_hi: 2, y_lo: 2; y = y_hi * 2 + y_lo), z: 16, core: 2. Of those that a mesh axis runs over, the one named last changes fastest.
Arguments:
- tokens: bfloat16 [1024, 3072], P('expert'), may hold values from -6 to 6
- routes: int32 [1024, 2], P('expert'), may hold values from 0 to 7, all different within a row; in each aligned block of 128 rows (0 to 127, 128 to 255, ...) at most 40 rows name the same one
- w_gate: bfloat16 [8, 3072, 8192], P('expert', None, 'etp'), may hold values from -0.3125 to 0.3125
- w_up: bfloat16 [8, 3072, 8192], P('expert', None, 'etp'), may hold values from -0.3125 to 0.3125
- d_hidden: bfloat16 [1024, 2, 8192], P('expert', None, 'etp'), may hold values from -6 to 6
Outputs:
- d_tokens: bfloat16 [1024, 3072], P('expert', 'etp')
- update_gate: bfloat16 [8, 3072, 8192], P('expert', None, 'etp')
- update_up: bfloat16 [8, 3072, 8192], P('expert', None, 'etp')
The draws below stay inside these ranges and needn't reach their ends.
Inputs may be any that keep to these rules, and one draw needn't show every extreme that they name: `routes`: in each aligned block of 128 rows (the tokens of one index of expert) a row names two different experts, no expert is named by more than 40 rows, a bound that some block reaches.
All inputs are finite; a program needn't handle non-finite values.
Results may differ from the reference program's by a relative error of at most 0.0055.
Values may be sent and summed in bfloat16 or wider, within the bound.
A program may use at most 64 MiB of HBM per device.

```python
import math
import jax
import jax.numpy as jnp
import numpy as np
from jax import lax

D = 3072
FF = 8192
NS_STEPS = 3
BLK = 128
TOK_DEV = 128
EXPERTS = 8
CAP = 40
TOKENS = 1024
N_EXPERT = 8


def spiked(entries, own_key, source, target, parts, factor):
    owner, partner = [(jnp.arange(entries.shape[dim]) // (entries.shape[dim] // parts)).reshape([-1 if axis == dim else 1 for axis in range(entries.ndim)]) for dim in (source, target)]
    chosen = jax.random.permutation(own_key, parts)[partner]
    strong = (owner == chosen) | (owner == (partner + parts // 2) % parts)
    return jnp.where(strong, factor * entries, entries)


def levels(own_key, shape, cuts, smallest, high):
    def one(dim, blocks):
        steps = jax.random.uniform(jax.random.fold_in(jax.random.fold_in(own_key, 6), dim), (blocks,), jnp.float32, smallest / len(cuts), high / len(cuts))
        return jnp.repeat(jnp.exp(steps), shape[dim] // blocks).reshape((-1,) + (1,) * (len(shape) - dim - 1))

    gain = one(*cuts[0])
    for cut in cuts[1:]:
        gain = gain * one(*cut)
    return gain


def shared_out(key, own, number, rows, number_of, top, reach, slope):
    sequence = jax.random.permutation(key, number_of)
    packed, ordinary = shares(number_of, rows * top, reach, slope, True), shares(number_of, rows * top, reach, slope, False)
    places = jnp.arange(number_of)

    def named(lengths, rotation):
        used = int((lengths > 0).sum())
        fixed = max(1, used // 4)
        passed = fixed + (places - fixed + rotation * (used - fixed)) % max(1, number_of - fixed)
        return jnp.zeros((number_of,), jnp.int32).at[sequence[jnp.where(places < fixed, places, passed)]].set(jnp.asarray(lengths, jnp.int32))

    lengths = jnp.where(number % 4 == 0, named(packed, number // 4), named(ordinary, number - number // 4 - 1))
    mixed = jax.random.permutation(jax.random.fold_in(own, 3), number_of)
    donor, taker = mixed[0:number_of // 2 * 2:2], mixed[1:number_of // 2 * 2:2]
    margin = jnp.minimum(lengths[donor] - 1, reach - lengths[taker]) // 2
    margin = jnp.where((donor == sequence[0]) | (taker == sequence[0]) | (lengths[taker] == 0), 0, jnp.maximum(margin, 0))
    passed = jax.random.randint(jax.random.fold_in(own, 4), (number_of // 2,), 0, 1 << 20) % (margin + 1)
    lengths = lengths.at[donor].add(-passed).at[taker].add(passed)
    labels = jnp.searchsorted(jnp.cumsum(lengths), jnp.arange(rows * top), side="right").astype(jnp.int32)
    listing = labels.reshape(top, rows).T
    listing = listing[jax.random.permutation(jax.random.fold_in(own, 1), rows)]
    rotation = jax.random.randint(jax.random.fold_in(own, 2), (rows, 1), 0, top)
    return jnp.take_along_axis(listing, (jnp.arange(top)[None, :] + rotation) % top, axis=1)


def shares(count, total, bound, skew, full):
    weights = [(1 << 20) // math.isqrt(grade ** skew) + 1 for grade in range(1, count + 1)]
    largest = bound if full else min(bound, max(-(-total // count), total * weights[0] // sum(weights)))
    least = 1 if total - largest >= count - 1 else 0
    holding, spare = [largest] + [least] * (count - 1), total - largest - least * (count - 1)
    while spare > 0:
        movable = [i for i in range(1, count) if holding[i] < largest] or [i for i in range(1, count) if holding[i] < bound]
        pool, remaining = sum([weights[i] for i in movable]), spare
        for i in movable:
            extra = min(bound - holding[i], max(1, remaining * weights[i] // pool), spare)
            holding[i] = holding[i] + extra
            spare = spare - extra
    return np.array(holding)


def bell_draw(own_key, shape, deviation, most, pieces=(), kind=jnp.bfloat16):
    entries = jax.random.normal(own_key, shape, jnp.float32) * deviation
    if len(pieces) > 0:
        entries = levels(own_key, shape, pieces, -0.22, 0.18) * entries
    return jnp.clip(entries, min=-most, max=most).astype(kind)


def heavy_noise(key, dims, scale, bound, cuts, heavy, held_as=jnp.bfloat16):
    drawn = scale * jax.random.normal(key, dims, jnp.float32)
    if cuts:
        drawn = drawn * levels(key, dims, cuts, -0.22, 0.18)
    return jnp.clip(spiked(drawn, jax.random.fold_in(key, 3), *heavy), -bound, bound).astype(held_as)


def setup_inputs(seed: int = 0) -> dict:
    streams_of = jax.random.split(jax.random.key(seed), 6)
    tokens = bell_draw(streams_of[0], (TOKENS, D), 1.0, 6.0, ((0, 8),))
    routes_keys = jax.random.split(jax.random.fold_in(streams_of[1], 1), TOKENS // TOK_DEV)
    routes_turns = jax.random.permutation(jax.random.fold_in(streams_of[1], 3), TOKENS // TOK_DEV)
    routes = jax.vmap(lambda own, number: shared_out(jax.random.fold_in(streams_of[1], 2), own, number, TOK_DEV, EXPERTS, 2, CAP, 2))(routes_keys, routes_turns).reshape((TOKENS, 2))
    w_gate = heavy_noise(streams_of[2], (EXPERTS, D, FF), D ** -0.5, 0.3125, ((0, 8), (2, 64)), (2, 1, 64, 4.0))
    w_up = heavy_noise(streams_of[3], (EXPERTS, D, FF), D ** -0.5, 0.3125, ((0, 8), (2, 64)), (2, 1, 64, 4.0))
    d_hidden = bell_draw(streams_of[4], (TOKENS, 2, FF), 1.0, 6.0, ((0, 8), (2, 64)))
    return {"tokens": tokens, "routes": routes, "w_gate": w_gate, "w_up": w_up, "d_hidden": d_hidden}


ns_first = 3.4445
ns_second = -4.775
ns_third = 2.0315

def routing(route_block, experts, capacity):
    choices_flat = route_block.reshape(-1).astype(jnp.int32)
    chosen = (choices_flat[:, None] == jnp.arange(experts, dtype=jnp.int32)[None, :]).astype(jnp.int32)
    earlier = jnp.cumsum(chosen, axis=0) - chosen
    position = lax.optimization_barrier(jnp.sum(earlier * chosen, axis=1))
    destination = choices_flat * capacity + position
    placing = (jnp.arange(experts * capacity, dtype=jnp.int32)[:, None] == destination[None, :]).astype(jnp.float32)
    return placing

def orthogonalize(gradient):
    squares = jnp.sum(gradient * gradient)
    current = gradient * lax.rsqrt(squares + 1e-06)
    for iteration in range(NS_STEPS):
        gram_matrix = lax.dot_general(current, current, (((0,), (0,)), ((), ())), precision=lax.Precision.HIGHEST, preferred_element_type=jnp.float32)
        mixing = ns_second * gram_matrix + ns_third * jnp.dot(gram_matrix, gram_matrix, precision=lax.Precision.HIGHEST)
        current = ns_first * current + jnp.dot(current, mixing, precision=lax.Precision.HIGHEST)
    return current.astype(jnp.bfloat16)

def blockwise(gradient):
    blocks = gradient.reshape(D, FF // BLK, BLK).transpose(1, 0, 2)
    done = lax.map(orthogonalize, blocks)
    return done.transpose(1, 0, 2).reshape(D, FF)

def expert_step(operands):
    slot_rows, slot_cotangent, gate_weight, up_weight = operands
    gate_act = jnp.dot(slot_rows, gate_weight, preferred_element_type=jnp.float32)
    up_act = jnp.dot(slot_rows, up_weight, preferred_element_type=jnp.float32)
    sigmoid_gate = jax.nn.sigmoid(gate_act)
    d_up = (slot_cotangent * gate_act * sigmoid_gate).astype(jnp.bfloat16)
    d_gate = (slot_cotangent * up_act * sigmoid_gate * (1.0 + gate_act * (1.0 - sigmoid_gate))).astype(jnp.bfloat16)
    contract_rows = (((0,), (0,)), ((), ()))
    grad_gate = lax.dot_general(slot_rows, d_gate, contract_rows, preferred_element_type=jnp.float32)
    grad_up = lax.dot_general(slot_rows, d_up, contract_rows, preferred_element_type=jnp.float32)
    contract_units = (((1,), (1,)), ((), ()))
    back_rows = lax.dot_general(d_gate, gate_weight, contract_units, preferred_element_type=jnp.float32)
    back_rows = back_rows + lax.dot_general(d_up, up_weight, contract_units, preferred_element_type=jnp.float32)
    return (back_rows, blockwise(grad_gate), blockwise(grad_up))

def reference(tokens, routes, w_gate, w_up, d_hidden):
    groups = N_EXPERT
    experts = EXPERTS
    token_blocks = tokens.reshape(groups, TOK_DEV, D)
    route_blocks = routes.reshape(groups, TOK_DEV, 2)
    placing = jax.vmap(lambda route_block: routing(route_block, experts, CAP))(route_blocks)
    per_token = placing.reshape(groups, experts * CAP, TOK_DEV, 2).sum(axis=3)
    rows_in = jnp.einsum('gst,gtd->gsd', per_token, token_blocks.astype(jnp.float32), precision=lax.Precision.HIGHEST).astype(jnp.bfloat16)
    cotangent_in = jnp.einsum('gsa,gaf->gsf', placing, d_hidden.reshape(groups, 2 * TOK_DEV, FF).astype(jnp.float32), precision=lax.Precision.HIGHEST).astype(jnp.bfloat16)
    rows_expert = rows_in.reshape(groups, experts, CAP, D).transpose(1, 0, 2, 3).reshape(experts, groups * CAP, D)
    cotangent_expert = cotangent_in.reshape(groups, experts, CAP, FF).transpose(1, 0, 2, 3).reshape(experts, groups * CAP, FF)
    back_rows, update_gate, update_up = lax.map(expert_step, (rows_expert, cotangent_expert, w_gate, w_up))
    back_groups = back_rows.reshape(experts, groups, CAP, D).transpose(1, 0, 2, 3).reshape(groups, experts * CAP, D)
    d_tokens = jnp.einsum('gst,gsd->gtd', per_token, back_groups, precision=lax.Precision.HIGHEST)
    d_tokens = d_tokens.reshape(TOKENS, D).astype(jnp.bfloat16)
    return (d_tokens, update_gate, update_up)
```

```python
import functools

import jax
import jax.numpy as jnp
from jax import lax
from jax.experimental import pallas as pl
from jax.experimental.pallas import tpu as pltpu
from jax.sharding import PartitionSpec as P

EXPERTS = 8
ZS = 16
BLK = 128
CAP = 40
SLOTS = EXPERTS * CAP
NSUB = 2
STARTS = (0, 128)
SIZES = (128, 112)

NS_FIRST = 3.4445
NS_SECOND = -4.775
NS_THIRD = 2.0315

MESH = pl.DeviceIdType.MESH
F32 = jnp.float32
BF16 = jnp.bfloat16


def dot(a, b):
    return jnp.dot(a, b, preferred_element_type=F32)


def dot_nt(a, b):
    return lax.dot_general(a, b, (((1,), (1,)), ((), ())), preferred_element_type=F32)


def dot_exact(a, b):
    return jnp.dot(a, b, precision=lax.Precision.HIGHEST, preferred_element_type=F32)


def kernel(
    tokens_ref,
    routes_ref,
    w_gate_ref,
    w_up_ref,
    dh_ref,
    d_tokens_ref,
    update_gate_ref,
    update_up_ref,
    tok,
    wcat,
    rows_out,
    land,
    cot_out,
    cot_land,
    srows,
    a_hi,
    a_lo,
    gram,
    mix,
    bt_own,
    bt_send,
    bt_recv,
    ring_out,
    ring_in,
    ret_out,
    ret_in,
    pmat,
    in_sem,
    s1_send,
    s1_recv,
    cot_send,
    cot_recv,
    z_send,
    z_recv,
    c0_send,
    c0_recv,
    c2_send,
    c2_recv,
    x_send,
    x_recv,
    ring_send,
    ring_recv,
    ret_send,
    ret_recv,
):
    expert = lax.axis_index("expert")
    p = lax.axis_index("etp")
    z = p // 4
    y = (p // 2) % 2
    core = p % 2
    width = tok.shape[1]
    half = width // 2

    def peer(o):
        return (expert + o) % EXPERTS

    core_mate = z * 4 + y * 2 + (1 - core)
    z_up = (p + 4) % (4 * ZS)
    z_down = (p + 4 * ZS - 4) % (4 * ZS)
    z_to = (p + 4 * ZS + 4 - 8 * core) % (4 * ZS)
    y_mate = z * 4 + (1 - y) * 2 + core

    own_q = 2 * (z % 2) + core
    mate_q = 2 * (z % 2) + (1 - core)
    zown_q = 2 * (1 - z % 2) + core
    zmate_q = 2 * (1 - z % 2) + (1 - core)
    quarters = (own_q, mate_q, zown_q, zmate_q)

    tok_copy = pltpu.make_async_copy(
        tokens_ref.at[:, pl.ds(pl.multiple_of(own_q * width, 128), width)], tok, in_sem.at[0]
    )
    wg_copy = pltpu.make_async_copy(w_gate_ref.at[0], wcat.at[:, pl.ds(0, BLK)], in_sem.at[1])
    wu_copy = pltpu.make_async_copy(w_up_ref.at[0], wcat.at[:, pl.ds(BLK, BLK)], in_sem.at[2])
    tok_copy.start()
    wg_copy.start()
    wu_copy.start()

    barrier = pltpu.get_barrier_semaphore()

    def greet(e, d):
        pl.semaphore_signal(
            barrier, inc=1, device_id={"expert": e, "etp": d}, device_id_type=MESH
        )

    greet(expert, core_mate)
    greet(expert, z_up)
    greet(expert, z_down)
    for o in range(1, EXPERTS):
        greet(peer(o), p)
    for o in range(EXPERTS):
        greet(peer(o), y_mate)

    lane = lax.broadcasted_iota(jnp.int32, (128, 128), 1)
    row = lax.broadcasted_iota(jnp.int32, (128, 128), 0)
    names_0 = jnp.where(lane == routes_ref[:, 0:1], 1.0, 0.0).T
    names_1 = jnp.where(lane == routes_ref[:, 1:2], 1.0, 0.0).T
    names = names_0 + names_1
    before = jnp.where(row < lane, 1.0, 0.0).astype(BF16)
    position = dot(names.astype(BF16), before)
    position = jnp.where(names > 0.5, position, -1.0)
    rowf = row.astype(F32)
    tall, first, second = [], [], []
    for e in range(EXPERTS):
        place = jnp.where(rowf == position[e : e + 1, :], 1.0, 0.0)
        pmat[e] = place.astype(BF16)
        place = place[:CAP]
        tall.append(place)
        first.append(place * names_0[e : e + 1, :])
        second.append(place * names_1[e : e + 1, :])
    tall = jnp.concatenate(tall, axis=0).astype(BF16)
    first = jnp.concatenate(first, axis=0).astype(BF16)
    second = jnp.concatenate(second, axis=0).astype(BF16)
    token_of = lax.broadcasted_iota(jnp.int32, (128, 256), 0)
    choice = lax.broadcasted_iota(jnp.int32, (128, 256), 1)
    even = jnp.where(choice == 2 * token_of, 1.0, 0.0).astype(BF16)
    odd = jnp.where(choice == 2 * token_of + 1, 1.0, 0.0).astype(BF16)
    placing = (dot(first, even) + dot(second, odd)).astype(BF16)
    cot = dot(placing, dh_ref[...])
    for e in range(EXPERTS):
        padded = jnp.concatenate(
            [cot[CAP * e : CAP * e + CAP], jnp.zeros((8, 128), F32)], axis=0
        )
        cot_out[e] = padded.astype(BF16)
    tok_copy.wait()
    placed = dot(tall, tok[...])
    for e in range(EXPERTS):
        rows = placed[CAP * e : CAP * e + CAP]
        rows_out[e] = jnp.concatenate([rows[:, :half], rows[:, half:]], axis=0).astype(BF16)

    pl.semaphore_wait(barrier, 3 + (EXPERTS - 1) + EXPERTS)

    sends = []

    def remote(src, dst, send_sem, recv_sem, e, d):
        copy = pltpu.make_async_remote_copy(
            src_ref=src,
            dst_ref=dst,
            send_sem=send_sem,
            recv_sem=recv_sem,
            device_id={"expert": e, "etp": d},
            device_id_type=MESH,
        )
        sends.append(copy)
        return copy

    stage1, cots, zfwd, c0fwd, c2fwd = {}, {}, {}, {}, {}
    for o in range(1, EXPERTS):
        stage1[o] = remote(
            rows_out.at[peer(o)], land.at[0, o], s1_send.at[o], s1_recv.at[o], peer(o), p
        )
        stage1[o].start()
    for o in range(1, EXPERTS):
        cots[o] = remote(
            cot_out.at[peer(o)], cot_land.at[o], cot_send.at[o], cot_recv.at[o], peer(o), p
        )
        cots[o].start()
    land[0, 0] = rows_out[expert]
    cot_land[0] = cot_out[expert]

    for o in range(EXPERTS):
        if o > 0:
            stage1[o].wait_recv()
        zfwd[o] = remote(
            land.at[0, o], land.at[2, o], z_send.at[o], z_recv.at[o], expert, z_to
        )
        zfwd[o].start()
        c0fwd[o] = remote(
            land.at[0, o], land.at[1, o], c0_send.at[o], c0_recv.at[o], expert, core_mate
        )
        c0fwd[o].start()

    def compact(r):
        for j in range(EXPERTS // 2):
            one = land[r, 2 * j].astype(F32)
            two = land[r, 2 * j + 1].astype(F32)
            left = jnp.concatenate([one[:CAP], two[:CAP]], axis=0)
            right = jnp.concatenate([one[CAP:], two[CAP:]], axis=0)
            srows[r, pl.ds(2 * CAP * j, 2 * CAP), pl.ds(0, half)] = left.astype(BF16)
            srows[r, pl.ds(2 * CAP * j, 2 * CAP), pl.ds(half, half)] = right.astype(BF16)

    def forward(r):
        at = pl.multiple_of(quarters[r] * width, 128)
        return dot(srows[r], wcat[pl.ds(at, width), :])

    wg_copy.wait()
    wu_copy.wait()
    compact(0)
    acts = forward(0)
    for o in range(EXPERTS):
        zfwd[o].wait_recv()
        c2fwd[o] = remote(
            land.at[2, o], land.at[3, o], c2_send.at[o], c2_recv.at[o], expert, core_mate
        )
        c2fwd[o].start()
    for o in range(EXPERTS):
        c0fwd[o].wait_recv()
    compact(1)
    acts = acts + forward(1)
    compact(2)
    acts = acts + forward(2)
    for o in range(EXPERTS):
        c2fwd[o].wait_recv()
    compact(3)
    acts = acts + forward(3)

    for o in range(1, EXPERTS):
        cots[o].wait_recv()
    cotangent = jnp.concatenate(
        [cot_land[o].astype(F32)[:CAP] for o in range(EXPERTS)], axis=0
    )
    gate_act, up_act = acts[:, :BLK], acts[:, BLK:]
    sig = jax.nn.sigmoid(gate_act)
    d_up = cotangent * gate_act * sig
    d_gate = cotangent * up_act * sig * (1.0 + gate_act * (1.0 - sig))
    d_both = jnp.concatenate([d_gate, d_up], axis=1)
    d_both = jnp.concatenate([d_both, jnp.zeros((384 - SLOTS, 2 * BLK), F32)], axis=0)
    d_t = d_both.T.astype(BF16)

    gz = z // 4
    groups = [(gz + 2) % 4, (gz + 3) % 4, (gz + 1) % 4, gz]
    lower = lax.broadcasted_iota(jnp.int32, (48, 128), 1) < 64
    swaps = []
    first_core = core == 0
    for g in range(4):
        at = pl.multiple_of(groups[g] * width, 128)
        back = dot(wcat[pl.ds(at, width), :], d_t)
        for i in range(4):
            part = back[192 * i : 192 * i + 192]
            parts = [part[48 * k : 48 * k + 48] for k in range(4)]
            for mine in (True, False):
                pick = []
                for k in range(2):
                    a, b = parts[2 * k], parts[2 * k + 1]
                    if not mine:
                        a, b = b, a
                    pick.append(jnp.where(first_core, a, b))
                folded = pick[0][:, 256:] + pltpu.roll(pick[1][:, 256:], 64, 1)
                whole = jnp.concatenate(
                    [pick[0][:, :128], pick[1][:, :128], pick[0][:, 128:256], pick[1][:, 128:256], folded],
                    axis=0,
                )
                if mine:
                    bt_own[groups[g] * 4 + i] = whole
                else:
                    bt_send[groups[g] * 4 + i] = whole.astype(BF16)
        swap = remote(
            bt_send.at[pl.ds(groups[g] * 4, 4)],
            bt_recv.at[pl.ds(groups[g] * 4, 4)],
            x_send.at[g],
            x_recv.at[g],
            expert,
            core_mate,
        )
        swap.start()
        swaps.append(swap)

    def grad_piece(r):
        grad = dot(d_t[:, :SLOTS], srows[r])
        hi = grad.astype(BF16)
        lo = (grad - hi.astype(F32)).astype(BF16)
        a_hi[r] = hi
        a_lo[r] = lo

    def gram_piece(r):
        hi, lo = a_hi[r], a_lo[r]
        if r == 0:
            gram[0] = dot_nt(hi, hi)
            gram[1] = dot_nt(hi, lo)
        else:
            gram[0] = gram[0] + dot_nt(hi, hi)
            gram[1] = gram[1] + dot_nt(hi, lo)

    wide_row = lax.broadcasted_iota(jnp.int32, (256, 256), 0)
    wide_lane = lax.broadcasted_iota(jnp.int32, (256, 256), 1)
    state = {}

    def ns_start():
        cross = gram[1]
        g = gram[0] + cross + cross.T
        g = jnp.where((wide_row < BLK) == (wide_lane < BLK), g, 0.0)
        diagonal = jnp.where(wide_row == wide_lane, g, 0.0)
        sum_gate = jnp.sum(diagonal[:BLK], keepdims=True)
        sum_up = jnp.sum(diagonal[BLK:], keepdims=True)
        scale = jnp.where(
            wide_row < BLK, lax.rsqrt(sum_gate + 1e-06), lax.rsqrt(sum_up + 1e-06)
        )
        state["scale"] = scale
        state["g"] = g * scale * scale

    def polynomial(g):
        square = dot_exact(g, g)
        return jnp.where(wide_row == wide_lane, NS_FIRST, 0.0) + NS_SECOND * g + NS_THIRD * square

    def ns_one():
        g = state["g"]
        poly = polynomial(g)
        state["m"] = poly
        state["g"] = dot_exact(dot_exact(g, poly), poly)

    def ns_two():
        g = state["g"]
        poly = polynomial(g)
        both = dot_exact(jnp.concatenate([state["m"], g], axis=0), poly)
        state["m"] = both[:256]
        state["g"] = dot_exact(both[256:], poly)

    def ns_three():
        m = dot_exact(state["m"], polynomial(state["g"])) * state["scale"]
        hi = m.astype(BF16)
        mix[0] = hi
        mix[1] = (m - hi.astype(F32)).astype(BF16)

    def update_piece(r):
        hi = a_hi[r]
        update = dot(mix[0], hi) + dot(mix[1], hi) + dot(mix[0], a_lo[r])
        update = update.T.astype(BF16)
        at = pl.multiple_of(quarters[r] * width, 128)
        update_gate_ref[0, pl.ds(at, width), :] = update[:, :BLK]
        update_up_ref[0, pl.ds(at, width), :] = update[:, BLK:]

    def both_pieces(r):
        grad_piece(r)
        gram_piece(r)

    tasks = [functools.partial(both_pieces, r) for r in range(4)]
    tasks += [ns_start, ns_one, ns_two, ns_three]
    tasks += [functools.partial(update_piece, r) for r in range(4)]
    plan = {0: 1, 1: 1, 2: 1, 3: 1, 4: 2, 5: 1, 6: 1, 7: 4}

    steps = ZS // 2
    up, down = {}, {}

    def send_chunk(which, slot, dst, previous, to):
        for i in range(NSUB):
            at = pl.ds(STARTS[i], SIZES[i])
            value = bt_own[dst, at] + bt_recv[dst, at].astype(F32)
            if previous is not None:
                previous[i].wait_recv()
                value = value + ring_in[slot - 1, at].astype(F32)
            ring_out[slot, at] = value.astype(BF16)
            copy = remote(
                ring_out.at[slot, at],
                ring_in.at[slot, at],
                ring_send.at[slot, i],
                ring_recv.at[slot, i],
                expert,
                to,
            )
            copy.start()
            which.setdefault(slot, []).append(copy)

    for s in range(steps):
        if s == 0:
            swaps[0].wait_recv()
            swaps[1].wait_recv()
        elif s == 1:
            swaps[2].wait_recv()
        elif s == 4:
            swaps[3].wait_recv()
        send_chunk(up, s, (z + steps - s) % ZS, up.get(s - 1), z_up)
        if s < steps - 1:
            slot = steps + s
            send_chunk(
                down, slot, (z + ZS - (steps - 1 - s)) % ZS, down.get(slot - 1), z_down
            )
        for _ in range(plan[s]):
            tasks.pop(0)()
    while tasks:
        tasks.pop(0)()
    pieces = []
    for i in range(NSUB):
        at = pl.ds(STARTS[i], SIZES[i])
        up[steps - 1][i].wait_recv()
        down[2 * steps - 2][i].wait_recv()
        pieces.append(
            bt_own[z, at]
            + bt_recv[z, at].astype(F32)
            + ring_in[steps - 1, at].astype(F32)
            + ring_in[2 * steps - 2, at].astype(F32)
        )
    total = jnp.concatenate(pieces, axis=0)
    folded = total[192:]
    tail = jnp.concatenate(
        [jnp.where(lower, folded, 0.0), jnp.where(lower, pltpu.roll(folded, 64, 1), 0.0)], axis=0
    )
    total = jnp.concatenate([total[:96], total[96:192], tail], axis=1).astype(BF16)
    slot_of = lax.broadcasted_iota(jnp.int32, (384, 128), 0)
    place_of = lax.broadcasted_iota(jnp.int32, (384, 128), 1)
    for o in range(EXPERTS):
        spread = jnp.where((slot_of == place_of + CAP * o) & (place_of < CAP), 1.0, 0.0)
        block = dot(total, spread.astype(BF16)).astype(BF16)
        ret_out[o, 0] = block[:48]
        ret_out[o, 1] = block[48:]

    returns = []
    for dy in range(2):
        to_y = (y + dy) % 2
        for o in range(EXPERTS):
            if o == 0 and dy == 0:
                continue
            copy = remote(
                ret_out.at[o, to_y],
                ret_in.at[o, dy],
                ret_send.at[o, dy],
                ret_recv.at[o, dy],
                (expert + EXPERTS - o) % EXPERTS,
                z * 4 + to_y * 2 + core,
            )
            copy.start()
            returns.append(copy)
    ret_in[0, 0] = ret_out[0, y]
    for copy in returns:
        copy.wait_recv()
    out = jnp.zeros((48, 128), F32)
    for o in range(EXPERTS):
        place = pmat[peer(o)]
        out = out + dot(ret_in[o, 0], place) + dot(ret_in[o, 1], place)
    out = jnp.concatenate([out, jnp.zeros((80, 128), F32)], axis=0).T
    d_tokens_ref[...] = out[:, :48].astype(BF16)
    for copy in sends:
        copy.wait_send()


def body(tokens, routes, w_gate, w_up, d_hidden):
    count, model_width = tokens.shape
    units = w_gate.shape[2]
    width = model_width // 4
    half = width // 2
    steps = ZS - 1
    dma = pltpu.SemaphoreType.DMA
    scratch = [
        pltpu.VMEM((count, width), BF16),
        pltpu.VMEM((model_width, 2 * units), BF16),
        pltpu.VMEM((EXPERTS, 2 * CAP, half), BF16),
        pltpu.VMEM((4, EXPERTS, 2 * CAP, half), BF16),
        pltpu.VMEM((EXPERTS, 48, units), BF16),
        pltpu.VMEM((EXPERTS, 48, units), BF16),
        pltpu.VMEM((4, SLOTS, width), BF16),
        pltpu.VMEM((4, 2 * units, width), BF16),
        pltpu.VMEM((4, 2 * units, width), BF16),
        pltpu.VMEM((2, 2 * units, 2 * units), F32),
        pltpu.VMEM((2, 2 * units, 2 * units), BF16),
        pltpu.VMEM((ZS, 240, 128), F32),
        pltpu.VMEM((ZS, 240, 128), BF16),
        pltpu.VMEM((ZS, 240, 128), BF16),
        pltpu.VMEM((steps, 240, 128), BF16),
        pltpu.VMEM((steps, 240, 128), BF16),
        pltpu.VMEM((EXPERTS, 2, 48, 128), BF16),
        pltpu.VMEM((EXPERTS, 2, 48, 128), BF16),
        pltpu.VMEM((EXPERTS, 128, 128), BF16),
        dma((3,)),
    ]
    for shape in ((EXPERTS,), (EXPERTS,), (EXPERTS,), (EXPERTS,), (EXPERTS,), (4,), (steps, NSUB), (EXPERTS, 2)):
        scratch += [dma(shape), dma(shape)]
    vmem = pl.BlockSpec(memory_space=pltpu.VMEM)
    anywhere = pl.BlockSpec(memory_space=pl.ANY)
    return pl.pallas_call(
        kernel,
        out_shape=(
            jax.ShapeDtypeStruct((count, 48), BF16),
            jax.ShapeDtypeStruct(w_gate.shape, BF16),
            jax.ShapeDtypeStruct(w_up.shape, BF16),
        ),
        in_specs=[anywhere, vmem, anywhere, anywhere, vmem],
        out_specs=(vmem, vmem, vmem),
        scratch_shapes=scratch,
        compiler_params=pltpu.CompilerParams(
            collective_id=0, has_side_effects=True, vmem_limit_bytes=56 * 1024 * 1024
        ),
    )(tokens, routes, w_gate, w_up, d_hidden.reshape(2 * count, units))


def solution(mesh):
    in_specs = (
        P("expert", None),
        P("expert", None),
        P("expert", None, "etp"),
        P("expert", None, "etp"),
        P("expert", None, "etp"),
    )
    out_specs = (P("expert", "etp"), P("expert", None, "etp"), P("expert", None, "etp"))
    return jax.shard_map(body, mesh=mesh, in_specs=in_specs, out_specs=out_specs, check_vma=False)
```

```python
import functools

import jax
import jax.numpy as jnp
from jax import lax
from jax.experimental import pallas as pl
from jax.experimental.pallas import tpu as pltpu
from jax.sharding import PartitionSpec as P

EXPERTS = 8
ZS = 16
BLK = 128
CAP = 40
SLOTS = EXPERTS * CAP
PARTS = 3
FAR_FIRST = (5, 3, 4, 7, 1, 6, 2)
ORDER = (8, 7, 9, 6, 10, 5, 11, 12, 4, 3, 13, 2, 14, 1, 15, 0)
WORK = (8, 3, 1)

NS_FIRST = 3.4445
NS_SECOND = -4.775
NS_THIRD = 2.0315

MESH = pl.DeviceIdType.MESH
F32 = jnp.float32
BF16 = jnp.bfloat16


def dot(a, b):
    return jnp.dot(a, b, preferred_element_type=F32)


def dot_nt(a, b):
    return lax.dot_general(a, b, (((1,), (1,)), ((), ())), preferred_element_type=F32)


def dot_exact(a, b):
    return jnp.dot(a, b, precision=lax.Precision.HIGHEST, preferred_element_type=F32)


def kernel(
    tokens_ref,
    routes_ref,
    w_gate_ref,
    w_up_ref,
    dh_ref,
    d_tokens_ref,
    update_gate_ref,
    update_up_ref,
    routes,
    tok,
    dh,
    updates,
    wcat,
    rows_out,
    land,
    cot_out,
    cot_land,
    srows,
    a_hi,
    a_lo,
    gram,
    mix,
    swap_out,
    swap_in,
    first_out,
    first_in,
    later_out,
    later_in,
    zx_out,
    zx_in,
    pmat,
    in_sem,
    out_sem,
    s1_send,
    s1_recv,
    cot_send,
    cot_recv,
    z_send,
    z_recv,
    c0_send,
    c0_recv,
    c2_send,
    c2_recv,
    swap_send,
    swap_recv,
    a2a_send,
    a2a_recv,
    zx_send,
    zx_recv,
):
    expert = lax.axis_index("expert")
    p = lax.axis_index("etp")
    z = p // 4
    y = (p // 2) % 2
    core = p % 2
    width = tok.shape[1]
    half = width // 2

    def peer(o):
        return (expert + o) % EXPERTS

    def back_peer(o):
        return (expert + EXPERTS - o) % EXPERTS

    core_mate = z * 4 + y * 2 + (1 - core)
    z_to = (p + 4 * ZS + 4 - 8 * core) % (4 * ZS)
    y_mate = z * 4 + (1 - y) * 2 + core

    def near(e):
        cross = (expert + e) % 2
        return z * 4 + ((y + cross) % 2) * 2 + core

    own_q = 2 * (z % 2) + core
    mate_q = 2 * (z % 2) + (1 - core)
    zown_q = 2 * (1 - z % 2) + core
    zmate_q = 2 * (1 - z % 2) + (1 - core)
    quarters = (own_q, mate_q, zown_q, zmate_q)

    tok_copy = pltpu.make_async_copy(
        tokens_ref.at[:, pl.ds(pl.multiple_of(own_q * width, 128), width)], tok, in_sem.at[0]
    )
    wg_copy = pltpu.make_async_copy(w_gate_ref.at[0], wcat.at[:, pl.ds(0, BLK)], in_sem.at[1])
    wu_copy = pltpu.make_async_copy(w_up_ref.at[0], wcat.at[:, pl.ds(BLK, BLK)], in_sem.at[2])
    dh_copy = pltpu.make_async_copy(dh_ref, dh, in_sem.at[3])
    routes_copy = pltpu.make_async_copy(routes_ref, routes, in_sem.at[4])
    routes_copy.start()
    tok_copy.start()
    dh_copy.start()
    wg_copy.start()
    wu_copy.start()

    barrier = pltpu.get_barrier_semaphore()

    def greet(e, d):
        pl.semaphore_signal(
            barrier, inc=1, device_id={"expert": e, "etp": d}, device_id_type=MESH
        )

    for o in range(1, EXPERTS):
        greet(peer(o), p)
    for o in range(EXPERTS):
        greet(peer(o), y_mate)
    greet(expert, core_mate)
    for dz in range(1, ZS):
        greet(expert, (p + 4 * dz) % (4 * ZS))

    lane = lax.broadcasted_iota(jnp.int32, (128, 128), 1)
    row = lax.broadcasted_iota(jnp.int32, (128, 128), 0)
    routes_copy.wait()
    names_0 = jnp.where(row == routes[0:1, :], 1.0, 0.0)
    names_1 = jnp.where(row == routes[1:2, :], 1.0, 0.0)
    names = names_0 + names_1
    before = jnp.where(row < lane, 1.0, 0.0).astype(BF16)
    position = dot(names.astype(BF16), before)
    position = jnp.where(names > 0.5, position, -1.0)
    slot = row[:CAP].astype(F32)
    places = []
    for e in range(EXPERTS):
        place = jnp.where(slot == position[e : e + 1, :], 1.0, 0.0)
        pmat[e] = place
        places.append(place)
    tok_copy.wait()
    placed = dot(jnp.concatenate(places, axis=0).astype(BF16), tok[...])
    for e in range(EXPERTS):
        rows = placed[CAP * e : CAP * e + CAP]
        for k in range(PARTS):
            left = rows[:, 128 * k : 128 * k + 128]
            right = rows[:, half + 128 * k : half + 128 * k + 128]
            rows_out[k, e] = jnp.concatenate([left, right], axis=0).astype(BF16)

    pl.semaphore_wait(barrier, (EXPERTS - 1) + EXPERTS + 1 + (ZS - 1))

    sends = []
    stores = []

    def finish():
        for copy in sends:
            copy.wait_send()
        for copy in stores:
            copy.wait()

    def remote(src, dst, send_sem, recv_sem, e, d):
        copy = pltpu.make_async_remote_copy(
            src_ref=src,
            dst_ref=dst,
            send_sem=send_sem,
            recv_sem=recv_sem,
            device_id={"expert": e, "etp": d},
            device_id_type=MESH,
        )
        copy.start()
        sends.append(copy)
        return copy

    stage1 = {}
    for k in range(PARTS):
        for o in FAR_FIRST:
            stage1[k, o] = remote(
                rows_out.at[k, peer(o)],
                land.at[0, k, o],
                s1_send.at[k, o],
                s1_recv.at[k, o],
                peer(o),
                near(peer(o)),
            )
    first = [places[e] * names_0[e : e + 1, :] for e in range(EXPERTS)]
    second = [places[e] * names_1[e : e + 1, :] for e in range(EXPERTS)]
    token_of = lax.broadcasted_iota(jnp.int32, (128, 256), 0)
    choice = lax.broadcasted_iota(jnp.int32, (128, 256), 1)
    even = jnp.where(choice == 2 * token_of, 1.0, 0.0).astype(BF16)
    odd = jnp.where(choice == 2 * token_of + 1, 1.0, 0.0).astype(BF16)
    placing = dot(jnp.concatenate(first, axis=0).astype(BF16), even)
    placing = placing + dot(jnp.concatenate(second, axis=0).astype(BF16), odd)
    dh_copy.wait()
    cot = dot(placing.astype(BF16), dh[...])
    for e in range(EXPERTS):
        padded = jnp.concatenate(
            [cot[CAP * e : CAP * e + CAP], jnp.zeros((8, 128), F32)], axis=0
        )
        cot_out[e] = padded.astype(BF16)
    cots = {}
    for o in FAR_FIRST:
        cots[o] = remote(
            cot_out.at[peer(o)], cot_land.at[o], cot_send.at[o], cot_recv.at[o], peer(o), p
        )
    for k in range(PARTS):
        land[0, k, 0] = rows_out[k, expert]
    cot_land[0] = cot_out[expert]
    gather = jnp.concatenate(
        [pmat[peer(o)] for o in range(EXPERTS) for _ in range(2)], axis=0
    ).T.astype(BF16)

    zfwd, c0fwd, c2fwd = {}, {}, {}
    for k in range(PARTS):
        for o in FAR_FIRST:
            stage1[k, o].wait_recv()
        zfwd[k] = remote(land.at[0, k], land.at[2, k], z_send.at[k], z_recv.at[k], expert, z_to)
        c0fwd[k] = remote(
            land.at[0, k], land.at[1, k], c0_send.at[k], c0_recv.at[k], expert, core_mate
        )

    def compact(r, k):
        for j in range(EXPERTS // 2):
            one = land[r, k, 2 * j].astype(F32)
            two = land[r, k, 2 * j + 1].astype(F32)
            left = jnp.concatenate([one[:CAP], two[:CAP]], axis=0)
            right = jnp.concatenate([one[CAP:], two[CAP:]], axis=0)
            at = pl.ds(2 * CAP * j, 2 * CAP)
            srows[r, at, pl.ds(128 * k, 128)] = left.astype(BF16)
            srows[r, at, pl.ds(half + 128 * k, 128)] = right.astype(BF16)

    def forward(r):
        at = pl.multiple_of(quarters[r] * width, 128)
        return dot(srows[r], wcat[pl.ds(at, width), :])

    for k in range(PARTS):
        compact(0, k)
    wg_copy.wait()
    wu_copy.wait()
    acts = forward(0)
    for k in range(PARTS):
        zfwd[k].wait_recv()
        c2fwd[k] = remote(
            land.at[2, k], land.at[3, k], c2_send.at[k], c2_recv.at[k], expert, core_mate
        )
        c0fwd[k].wait_recv()
        compact(1, k)
        compact(2, k)
        if k == PARTS - 2:
            for o in FAR_FIRST:
                cots[o].wait_recv()
            cotangent = jnp.concatenate(
                [cot_land[o].astype(F32)[:CAP] for o in range(EXPERTS)], axis=0
            )
    acts = acts + forward(1)
    acts = acts + forward(2)
    for k in range(PARTS):
        c2fwd[k].wait_recv()
        compact(3, k)
    acts = acts + forward(3)

    gate_act, up_act = acts[:, :BLK], acts[:, BLK:]
    sig = jax.nn.sigmoid(gate_act)
    d_up = cotangent * gate_act * sig
    d_gate = cotangent * up_act * sig * (1.0 + gate_act * (1.0 - sig))
    d_both = jnp.concatenate([d_gate, d_up], axis=1)
    d_rows = d_both.astype(BF16)
    d_both = jnp.concatenate([d_both, jnp.zeros((384 - SLOTS, 2 * BLK), F32)], axis=0)
    d_t = d_both.T.astype(BF16)[:, :SLOTS]

    def grad_piece(r):
        grad = dot(d_t, srows[r])
        hi = grad.astype(BF16)
        lo = (grad - hi.astype(F32)).astype(BF16)
        a_hi[r] = hi
        a_lo[r] = lo
        if r == 0:
            gram[0] = dot_nt(hi, hi)
            gram[1] = dot_nt(hi, lo)
        else:
            gram[0] = gram[0] + dot_nt(hi, hi)
            gram[1] = gram[1] + dot_nt(hi, lo)

    wide_row = lax.broadcasted_iota(jnp.int32, (256, 256), 0)
    wide_lane = lax.broadcasted_iota(jnp.int32, (256, 256), 1)
    state = {}

    def ns_start():
        cross = gram[1]
        g = gram[0] + cross + cross.T
        g = jnp.where((wide_row < BLK) == (wide_lane < BLK), g, 0.0)
        diagonal = jnp.where(wide_row == wide_lane, g, 0.0)
        sum_gate = jnp.sum(diagonal[:BLK], keepdims=True)
        sum_up = jnp.sum(diagonal[BLK:], keepdims=True)
        scale = jnp.where(
            wide_row < BLK, lax.rsqrt(sum_gate + 1e-06), lax.rsqrt(sum_up + 1e-06)
        )
        state["scale"] = scale
        state["g"] = g * scale * scale

    def polynomial(g):
        square = dot_exact(g, g)
        return jnp.where(wide_row == wide_lane, NS_FIRST, 0.0) + NS_SECOND * g + NS_THIRD * square

    def ns_one():
        g = state["g"]
        poly = polynomial(g)
        state["m"] = poly
        state["g"] = dot_exact(dot_exact(g, poly), poly)

    def ns_two():
        g = state["g"]
        poly = polynomial(g)
        both = dot_exact(jnp.concatenate([state["m"], g], axis=0), poly)
        state["m"] = both[:256]
        state["g"] = dot_exact(both[256:], poly)

    def ns_three():
        m = dot_exact(state["m"], polynomial(state["g"])) * state["scale"]
        hi = m.astype(BF16)
        mix[0] = hi
        mix[1] = (m - hi.astype(F32)).astype(BF16)

    def update_piece(r):
        hi = a_hi[r]
        update = dot(mix[0], hi) + dot(mix[1], hi) + dot(mix[0], a_lo[r])
        update = update.T.astype(BF16)
        at = pl.multiple_of(quarters[r] * width, 128)
        for k, out_ref in enumerate((update_gate_ref, update_up_ref)):
            updates[k, r] = update[:, BLK * k : BLK * k + BLK]
            copy = pltpu.make_async_copy(
                updates.at[k, r], out_ref.at[0, pl.ds(at, width)], out_sem.at[k, r]
            )
            copy.start()
            stores.append(copy)

    def back(st, which):
        rows = []
        for side in range(2):
            for dz in ORDER[8 * st : 8 * st + 8]:
                at = ((z + dz) % ZS) * 192 + side * 96 + which * 48
                rows.append(wcat[pl.ds(pl.multiple_of(at, 16), 48), :])
        return dot_nt(d_rows, jnp.concatenate(rows, axis=0))

    tasks = [functools.partial(grad_piece, r) for r in range(4)]
    tasks += [ns_start, ns_one, ns_two, ns_three]
    tasks += [functools.partial(update_piece, r) for r in range(4)]

    def work(count):
        for _ in range(count):
            if tasks:
                tasks.pop(0)()

    swaps = []
    for st in range(2):
        swap_out[st] = back(st, 1 - core).astype(BF16)
        swaps.append(
            remote(
                swap_out.at[st],
                swap_in.at[st],
                swap_send.at[st],
                swap_recv.at[st],
                expert,
                core_mate,
            )
        )
    totals = []
    for st in range(2):
        totals.append(back(st, core))
    for st in range(2):
        swaps[st].wait_recv()
        totals[st] = totals[st] + swap_in[st].astype(F32)

    returns = {}
    for st in range(2):
        out_ref, in_ref = ((first_out, first_in), (later_out, later_in))[st]
        for o in FAR_FIRST + (0,):
            low, high = CAP * o, CAP * o + CAP
            for side in range(2):
                cols = slice(half * side, half * side + half)
                if st == 0:
                    block = jnp.concatenate(
                        [totals[0][low:high, cols], totals[1][high - 8 : high, cols]], axis=0
                    )
                else:
                    block = totals[1][low : high - 8, cols]
                out_ref[o, side] = block.astype(BF16)
            for dy in (1, 0):
                to_y = (y + dy) % 2
                if o == 0 and dy == 0:
                    in_ref[0, 0] = out_ref[0, y]
                    continue
                returns[st, o, dy] = remote(
                    out_ref.at[o, to_y],
                    in_ref.at[o, dy],
                    a2a_send.at[st, o, dy],
                    a2a_recv.at[st, o, dy],
                    back_peer(o),
                    z * 4 + to_y * 2 + core,
                )
    copies = {}
    for st in range(2):
        work(WORK[st])
        got = []
        for o in range(EXPERTS):
            for dy in range(2):
                if (st, o, dy) in returns:
                    returns[st, o, dy].wait_recv()
                first = first_in[o, dy].astype(F32)
                if st == 0:
                    got.append(first[:CAP])
                else:
                    got.append(later_in[o, dy].astype(F32))
                    got.append(first[CAP:])
        part = dot(gather, jnp.concatenate(got, axis=0).astype(BF16)).T
        for i in range(8):
            dz = ORDER[8 * st + i]
            value = part[48 * i : 48 * i + 48]
            if dz == 0:
                mine = value
                continue
            zx_out[dz] = value.astype(BF16)
            copies[dz] = remote(
                zx_out.at[dz],
                zx_in.at[dz],
                zx_send.at[dz],
                zx_recv.at[dz],
                expert,
                (p + 4 * dz) % (4 * ZS),
            )
    work(len(tasks))
    for dz, copy in copies.items():
        copy.wait_recv()
        mine = mine + zx_in[dz].astype(F32)
    d_tokens_ref[...] = mine.astype(BF16)
    finish()


def hand_on(parts, t_ref, a_ref, b_ref, t_out, a_out, b_out, t_held, held, in_sem, out_sem):
    rows = a_ref.shape[1] // parts
    moves = [(t_ref, t_held, t_out, in_sem.at[0, parts], out_sem.at[0, parts])]
    for i in range(parts):
        at = pl.ds(i * rows, rows)
        for k, (src, dst) in enumerate(((a_ref, a_out), (b_ref, b_out))):
            moves.append(
                (src.at[0, at], held.at[k, at], dst.at[0, at], in_sem.at[k, i], out_sem.at[k, i])
            )
    loads = [pltpu.make_async_copy(src, mid, sem) for src, mid, _, sem, _ in moves]
    stores = [pltpu.make_async_copy(mid, dst, sem) for _, mid, dst, _, sem in moves]
    for load in loads:
        load.start()
    for load, store in zip(loads, stores):
        load.wait()
        store.start()
    for store in stores:
        store.wait()


def body(tokens, routes, w_gate, w_up, d_hidden):
    count, model_width = tokens.shape
    units = w_gate.shape[2]
    width = model_width // 4
    half = width // 2
    dma = pltpu.SemaphoreType.DMA
    scratch = [
        pltpu.VMEM((2, count), jnp.int32),
        pltpu.VMEM((count, width), BF16),
        pltpu.VMEM((2 * count, units), BF16),
        pltpu.VMEM((2, 4, width, units), BF16),
        pltpu.VMEM((model_width, 2 * units), BF16),
        pltpu.VMEM((PARTS, EXPERTS, 2 * CAP, 128), BF16),
        pltpu.VMEM((4, PARTS, EXPERTS, 2 * CAP, 128), BF16),
        pltpu.VMEM((EXPERTS, 48, units), BF16),
        pltpu.VMEM((EXPERTS, 48, units), BF16),
        pltpu.VMEM((4, SLOTS, width), BF16),
        pltpu.VMEM((4, 2 * units, width), BF16),
        pltpu.VMEM((4, 2 * units, width), BF16),
        pltpu.VMEM((2, 2 * units, 2 * units), F32),
        pltpu.VMEM((2, 2 * units, 2 * units), BF16),
        pltpu.VMEM((2, SLOTS, width), BF16),
        pltpu.VMEM((2, SLOTS, width), BF16),
        pltpu.VMEM((EXPERTS, 2, CAP + 8, half), BF16),
        pltpu.VMEM((EXPERTS, 2, CAP + 8, half), BF16),
        pltpu.VMEM((EXPERTS, 2, CAP - 8, half), BF16),
        pltpu.VMEM((EXPERTS, 2, CAP - 8, half), BF16),
        pltpu.VMEM((ZS, 48, count), BF16),
        pltpu.VMEM((ZS, 48, count), BF16),
        pltpu.VMEM((EXPERTS, CAP, count), F32),
        dma((5,)),
        dma((2, 4)),
    ]
    for shape in (
        (PARTS, EXPERTS),
        (EXPERTS,),
        (PARTS,),
        (PARTS,),
        (PARTS,),
        (2,),
        (2, EXPERTS, 2),
        (ZS,),
    ):
        scratch += [dma(shape), dma(shape)]
    vmem = pl.BlockSpec(memory_space=pltpu.VMEM)
    anywhere = pl.BlockSpec(memory_space=pl.ANY)
    d_tokens, update_gate, update_up = pl.pallas_call(
        kernel,
        out_shape=(
            jax.ShapeDtypeStruct((48, count), BF16),
            jax.ShapeDtypeStruct(w_gate.shape, BF16),
            jax.ShapeDtypeStruct(w_up.shape, BF16),
        ),
        in_specs=[anywhere] * 5,
        out_specs=(vmem, anywhere, anywhere),
        scratch_shapes=scratch,
        compiler_params=pltpu.CompilerParams(
            collective_id=0, has_side_effects=True, vmem_limit_bytes=56 * 1024 * 1024
        ),
    )(tokens, routes.T, w_gate, w_up, d_hidden.reshape(2 * count, units))
    parts = 4
    d_tokens, update_gate, update_up = pl.pallas_call(
        functools.partial(hand_on, parts),
        out_shape=(
            jax.ShapeDtypeStruct((48, count), BF16),
            jax.ShapeDtypeStruct(w_gate.shape, BF16),
            jax.ShapeDtypeStruct(w_up.shape, BF16),
        ),
        in_specs=[anywhere] * 3,
        out_specs=(anywhere,) * 3,
        scratch_shapes=[
            pltpu.VMEM((48, count), BF16),
            pltpu.VMEM((2, model_width, units), BF16),
            dma((2, parts + 1)),
            dma((2, parts + 1)),
        ],
    )(d_tokens, update_gate, update_up)
    return d_tokens.T, update_gate, update_up


def solution(mesh):
    in_specs = (
        P("expert", None),
        P("expert", None),
        P("expert", None, "etp"),
        P("expert", None, "etp"),
        P("expert", None, "etp"),
    )
    out_specs = (P("expert", "etp"), P("expert", None, "etp"), P("expert", None, "etp"))
    return jax.shard_map(body, mesh=mesh, in_specs=in_specs, out_specs=out_specs, check_vma=False)
```

```python
import functools

import jax
import jax.numpy as jnp
from jax import lax
from jax.experimental import pallas as pl
from jax.experimental.pallas import tpu as pltpu
from jax.sharding import PartitionSpec as P

EXPERTS = 8
ZS = 16
BLK = 128
CAP = 40
SLOTS = EXPERTS * CAP
PARTS = 3
FAR_FIRST = (5, 3, 4, 7, 1, 6, 2)
GROUPS = ((0, 1, 2, 3), (4, 5, 6, 7))
ORDER = (8, 7, 9, 6, 10, 5, 11, 4, 12, 3, 13, 2, 14, 1, 15, 0)
STAGES = 3
OWNED = 48
WORK = (8, 2, 1)

NS_FIRST = 3.4445
NS_SECOND = -4.775
NS_THIRD = 2.0315

MESH = pl.DeviceIdType.MESH
F32 = jnp.float32
BF16 = jnp.bfloat16


def dot(a, b):
    return jnp.dot(a, b, preferred_element_type=F32)


def dot_nt(a, b):
    return lax.dot_general(a, b, (((1,), (1,)), ((), ())), preferred_element_type=F32)


def dot_exact(a, b):
    return jnp.dot(a, b, precision=lax.Precision.HIGHEST, preferred_element_type=F32)


def kernel(
    tokens_ref,
    routes_ref,
    w_gate_ref,
    w_up_ref,
    dh_ref,
    d_tokens_ref,
    update_gate_ref,
    update_up_ref,
    routes,
    tok,
    dh,
    updates,
    wcat,
    rows_out,
    land,
    cot_out,
    cot_land,
    srows,
    a_hi,
    a_lo,
    gram,
    mix,
    w_own,
    w_out,
    w_in,
    d_out,
    d_in,
    out_0,
    in_0,
    out_1,
    in_1,
    out_2,
    in_2,
    zx_out,
    zx_in,
    pmat,
    known,
    in_sem,
    out_sem,
    s1_send,
    s1_recv,
    cot_send,
    cot_recv,
    z_send,
    z_recv,
    c0_send,
    c0_recv,
    c2_send,
    c2_recv,
    swap_send,
    swap_recv,
    a2a_send,
    a2a_recv,
    zx_send,
    zx_recv,
):
    expert = lax.axis_index("expert")
    p = lax.axis_index("etp")
    z = p // 4
    y = (p // 2) % 2
    core = p % 2
    width = tok.shape[1]
    half = width // 2

    def peer(o):
        return (expert + o) % EXPERTS

    def back_peer(o):
        return (expert + EXPERTS - o) % EXPERTS

    core_mate = z * 4 + y * 2 + (1 - core)
    z_to = (p + 4 * ZS + 4 - 8 * core) % (4 * ZS)
    y_mate = z * 4 + (1 - y) * 2 + core

    def near(e):
        cross = (expert + e) % 2
        return z * 4 + ((y + cross) % 2) * 2 + core

    own_q = 2 * (z % 2) + core
    mate_q = 2 * (z % 2) + (1 - core)
    zown_q = 2 * (1 - z % 2) + core
    zmate_q = 2 * (1 - z % 2) + (1 - core)
    quarters = (own_q, mate_q, zown_q, zmate_q)

    tok_copy = pltpu.make_async_copy(
        tokens_ref.at[:, pl.ds(pl.multiple_of(own_q * width, 128), width)], tok, in_sem.at[0]
    )
    wg_copy = pltpu.make_async_copy(w_gate_ref.at[0], wcat.at[:, pl.ds(0, BLK)], in_sem.at[1])
    wu_copy = pltpu.make_async_copy(w_up_ref.at[0], wcat.at[:, pl.ds(BLK, BLK)], in_sem.at[2])
    dh_copy = pltpu.make_async_copy(dh_ref, dh, in_sem.at[3])
    routes_copy = pltpu.make_async_copy(routes_ref, routes, in_sem.at[4])
    routes_copy.start()
    tok_copy.start()
    dh_copy.start()
    wg_copy.start()
    wu_copy.start()

    barrier = pltpu.get_barrier_semaphore()

    def greet(e, d):
        pl.semaphore_signal(
            barrier, inc=1, device_id={"expert": e, "etp": d}, device_id_type=MESH
        )

    for o in range(1, EXPERTS):
        greet(peer(o), p)
    for o in range(EXPERTS):
        greet(peer(o), y_mate)
    greet(expert, core_mate)
    for dz in (1, ZS - 1):
        greet(expert, (p + 4 * dz) % (4 * ZS))

    lane = lax.broadcasted_iota(jnp.int32, (128, 128), 1)
    row = lax.broadcasted_iota(jnp.int32, (128, 128), 0)
    routes_copy.wait()
    names_0 = jnp.where(row == routes[0:1, :], 1.0, 0.0)
    names_1 = jnp.where(row == routes[1:2, :], 1.0, 0.0)
    names = names_0 + names_1
    before = jnp.where(row < lane, 1.0, 0.0).astype(BF16)
    position = dot(names.astype(BF16), before)
    position = jnp.where(names > 0.5, position, -1.0)
    slot = row[:CAP].astype(F32)
    places = []
    for e in range(EXPERTS):
        place = jnp.where(slot == position[e : e + 1, :], 1.0, 0.0)
        pmat[e] = place
        places.append(place)
    tok_copy.wait()
    placed = dot(jnp.concatenate(places, axis=0).astype(BF16), tok[...])
    for e in range(EXPERTS):
        rows = placed[CAP * e : CAP * e + CAP]
        for k in range(PARTS):
            left = rows[:, 128 * k : 128 * k + 128]
            right = rows[:, half + 128 * k : half + 128 * k + 128]
            rows_out[k, e] = jnp.concatenate([left, right], axis=0).astype(BF16)

    pl.semaphore_wait(barrier, (EXPERTS - 1) + EXPERTS + 1 + 2)

    sends = []
    stores = []

    def finish():
        for copy in sends:
            copy.wait_send()
        for copy in stores:
            copy.wait()

    def remote(src, dst, send_sem, recv_sem, e, d):
        copy = pltpu.make_async_remote_copy(
            src_ref=src,
            dst_ref=dst,
            send_sem=send_sem,
            recv_sem=recv_sem,
            device_id={"expert": e, "etp": d},
            device_id_type=MESH,
        )
        copy.start()
        sends.append(copy)
        return copy

    def tell(step):
        for dz in (1 << step, ZS - (1 << step)):
            pl.semaphore_signal(
                known.at[step],
                inc=1,
                device_id={"expert": expert, "etp": (p + 4 * dz) % (4 * ZS)},
                device_id_type=MESH,
            )

    def hear(step):
        pl.semaphore_wait(known.at[step], 2)

    stage1 = {}
    for k in range(PARTS):
        for o in range(1, EXPERTS):
            stage1[k, o] = remote(
                rows_out.at[k, peer(o)],
                land.at[0, k, o],
                s1_send.at[k, o],
                s1_recv.at[k, o],
                peer(o),
                near(peer(o)),
            )
    tell(0)
    first = [places[e] * names_0[e : e + 1, :] for e in range(EXPERTS)]
    second = [places[e] * names_1[e : e + 1, :] for e in range(EXPERTS)]
    token_of = lax.broadcasted_iota(jnp.int32, (128, 256), 0)
    choice = lax.broadcasted_iota(jnp.int32, (128, 256), 1)
    even = jnp.where(choice == 2 * token_of, 1.0, 0.0).astype(BF16)
    odd = jnp.where(choice == 2 * token_of + 1, 1.0, 0.0).astype(BF16)
    placing = dot(jnp.concatenate(first, axis=0).astype(BF16), even)
    placing = placing + dot(jnp.concatenate(second, axis=0).astype(BF16), odd)
    dh_copy.wait()
    cot = dot(placing.astype(BF16), dh[...])
    for e in range(EXPERTS):
        padded = jnp.concatenate(
            [cot[CAP * e : CAP * e + CAP], jnp.zeros((8, 128), F32)], axis=0
        )
        cot_out[e] = padded.astype(BF16)
    cots = {}
    for o in FAR_FIRST:
        cots[o] = remote(
            cot_out.at[peer(o)], cot_land.at[o], cot_send.at[o], cot_recv.at[o], peer(o), p
        )
    for k in range(PARTS):
        land[0, k, 0] = rows_out[k, expert]
    cot_land[0] = cot_out[expert]
    gather = jnp.concatenate(
        [pmat[peer(o)] for o in range(EXPERTS) for _ in range(2)], axis=0
    ).T.astype(BF16)

    def compact(r, k):
        for j in range(EXPERTS // 2):
            one = land[r, k, 2 * j].astype(F32)
            two = land[r, k, 2 * j + 1].astype(F32)
            left = jnp.concatenate([one[:CAP], two[:CAP]], axis=0)
            right = jnp.concatenate([one[CAP:], two[CAP:]], axis=0)
            at = pl.ds(2 * CAP * j, 2 * CAP)
            srows[r, at, pl.ds(128 * k, 128)] = left.astype(BF16)
            srows[r, at, pl.ds(half + 128 * k, 128)] = right.astype(BF16)

    zfwd, c0fwd, c2fwd = {}, {}, {}

    def pass_on(copies, k, g, src, dst, send_sem, recv_sem, d):
        at = pl.ds(GROUPS[g][0], len(GROUPS[g]))
        copies[k, g] = remote(
            land.at[src, k, at],
            land.at[dst, k, at],
            send_sem.at[k, g],
            recv_sem.at[k, g],
            expert,
            d,
        )

    for k in range(PARTS):
        for g, members in enumerate(GROUPS):
            for o in members:
                if o > 0:
                    stage1[k, o].wait_recv()
            pass_on(zfwd, k, g, 0, 2, z_send, z_recv, z_to)
            pass_on(c0fwd, k, g, 0, 1, c0_send, c0_recv, core_mate)
        compact(0, k)

    def forward(r):
        at = pl.multiple_of(quarters[r] * width, 128)
        return dot(srows[r], wcat[pl.ds(at, width), :])

    def sort_weights(out_ref, which):
        for side in range(2):
            for i, dz in enumerate(ORDER):
                at = ((z + dz) % ZS) * 192 + side * 96 + which * OWNED
                out_ref[side, pl.ds(OWNED * i, OWNED), :] = wcat[
                    pl.ds(pl.multiple_of(at, 16), OWNED), :
                ]

    wg_copy.wait()
    wu_copy.wait()
    sort_weights(w_out, 1 - core)
    w_swap = remote(w_out, w_in, swap_send.at[0], swap_recv.at[0], expert, core_mate)
    sort_weights(w_own, core)
    hear(0)
    tell(1)
    acts = forward(0)
    for k in range(PARTS):
        for g in range(len(GROUPS)):
            zfwd[k, g].wait_recv()
            pass_on(c2fwd, k, g, 2, 3, c2_send, c2_recv, core_mate)
        for g in range(len(GROUPS)):
            c0fwd[k, g].wait_recv()
        compact(1, k)
        compact(2, k)
        if k == PARTS - 2:
            for o in FAR_FIRST:
                cots[o].wait_recv()
            cotangent = jnp.concatenate(
                [cot_land[o].astype(F32)[:CAP] for o in range(EXPERTS)], axis=0
            )
    hear(1)
    tell(2)
    acts = acts + forward(1)
    acts = acts + forward(2)
    for k in range(PARTS):
        for g in range(len(GROUPS)):
            c2fwd[k, g].wait_recv()
        compact(3, k)
    acts = acts + forward(3)

    gate_act, up_act = acts[:, :BLK], acts[:, BLK:]
    sig = jax.nn.sigmoid(gate_act)
    d_up = cotangent * gate_act * sig
    d_gate = cotangent * up_act * sig * (1.0 + gate_act * (1.0 - sig))
    d_both = jnp.concatenate([d_gate, d_up], axis=1)
    d_rows = d_both.astype(BF16)
    d_out[...] = d_rows
    d_swap = remote(d_out, d_in, swap_send.at[1], swap_recv.at[1], expert, core_mate)
    d_both = jnp.concatenate([d_both, jnp.zeros((384 - SLOTS, 2 * BLK), F32)], axis=0)
    d_t = d_both.T.astype(BF16)[:, :SLOTS]

    def grad_piece(r):
        grad = dot(d_t, srows[r])
        hi = grad.astype(BF16)
        lo = (grad - hi.astype(F32)).astype(BF16)
        a_hi[r] = hi
        a_lo[r] = lo
        if r == 0:
            gram[0] = dot_nt(hi, hi)
            gram[1] = dot_nt(hi, lo)
        else:
            gram[0] = gram[0] + dot_nt(hi, hi)
            gram[1] = gram[1] + dot_nt(hi, lo)

    wide_row = lax.broadcasted_iota(jnp.int32, (256, 256), 0)
    wide_lane = lax.broadcasted_iota(jnp.int32, (256, 256), 1)
    state = {}

    def ns_start():
        cross = gram[1]
        g = gram[0] + cross + cross.T
        g = jnp.where((wide_row < BLK) == (wide_lane < BLK), g, 0.0)
        diagonal = jnp.where(wide_row == wide_lane, g, 0.0)
        sum_gate = jnp.sum(diagonal[:BLK], keepdims=True)
        sum_up = jnp.sum(diagonal[BLK:], keepdims=True)
        scale = jnp.where(
            wide_row < BLK, lax.rsqrt(sum_gate + 1e-06), lax.rsqrt(sum_up + 1e-06)
        )
        state["scale"] = scale
        state["g"] = g * scale * scale

    def polynomial(g):
        square = dot_exact(g, g)
        return jnp.where(wide_row == wide_lane, NS_FIRST, 0.0) + NS_SECOND * g + NS_THIRD * square

    def ns_one():
        g = state["g"]
        poly = polynomial(g)
        state["m"] = poly
        state["g"] = dot_exact(dot_exact(g, poly), poly)

    def ns_two():
        g = state["g"]
        poly = polynomial(g)
        both = dot_exact(jnp.concatenate([state["m"], g], axis=0), poly)
        state["m"] = both[:256]
        state["g"] = dot_exact(both[256:], poly)

    def ns_three():
        m = dot_exact(state["m"], polynomial(state["g"])) * state["scale"]
        hi = m.astype(BF16)
        mix[0] = hi
        mix[1] = (m - hi.astype(F32)).astype(BF16)

    def update_piece(r):
        hi = a_hi[r]
        update = dot(mix[0], hi) + dot(mix[1], hi) + dot(mix[0], a_lo[r])
        update = update.T.astype(BF16)
        at = pl.multiple_of(quarters[r] * width, 128)
        for k, out_ref in enumerate((update_gate_ref, update_up_ref)):
            updates[k, r] = update[:, BLK * k : BLK * k + BLK]
            copy = pltpu.make_async_copy(
                updates.at[k, r], out_ref.at[0, pl.ds(at, width)], out_sem.at[k, r]
            )
            copy.start()
            stores.append(copy)

    tasks = [functools.partial(grad_piece, r) for r in range(4)]
    tasks += [ns_start, ns_one, ns_two, ns_three]
    tasks += [functools.partial(update_piece, r) for r in range(4)]

    def work(count):
        for _ in range(count):
            if tasks:
                tasks.pop(0)()

    cols = width // STAGES

    def back(rows, weights, st):
        at = pl.ds(cols * st, cols)
        return dot_nt(rows, jnp.concatenate([weights[0, at], weights[1, at]], axis=0))

    totals = [back(d_rows, w_own, st) for st in range(STAGES)]
    w_swap.wait_recv()
    d_swap.wait_recv()
    d_mate = d_in[...]

    returns = {}
    for st in range(STAGES):
        for more in {0: (0, 1), 1: (), 2: (2,)}[st]:
            totals[more] = totals[more] + back(d_mate, w_in, more)
        out_ref, in_ref = ((out_0, in_0), (out_1, in_1), (out_2, in_2))[st]
        for o in FAR_FIRST + (0,):
            low, high = CAP * o, CAP * o + CAP
            for side in range(2):
                cut = slice(cols * side, cols * side + cols)
                if st == 0:
                    block = [totals[0][low:high, cut], totals[1][high - 8 : high, cut]]
                elif st == 1:
                    block = [totals[1][low : high - 8, cut]]
                else:
                    block = [totals[2][low:high, cut], jnp.zeros((8, cols), F32)]
                out_ref[o, side] = jnp.concatenate(block, axis=0).astype(BF16)
            for dy in (1, 0):
                to_y = (y + dy) % 2
                if o == 0 and dy == 0:
                    in_ref[0, 0] = out_ref[0, y]
                    continue
                returns[st, o, dy] = remote(
                    out_ref.at[o, to_y],
                    in_ref.at[o, dy],
                    a2a_send.at[st, o, dy],
                    a2a_recv.at[st, o, dy],
                    back_peer(o),
                    z * 4 + to_y * 2 + core,
                )
    hear(2)
    copies = {}
    for st in range(STAGES):
        work(WORK[st])
        got = []
        for o in range(EXPERTS):
            for dy in range(2):
                if (st, o, dy) in returns:
                    returns[st, o, dy].wait_recv()
                if st == 0:
                    got.append(in_0[o, dy].astype(F32)[:CAP])
                elif st == 1:
                    got.append(in_1[o, dy].astype(F32))
                    got.append(in_0[o, dy].astype(F32)[CAP:])
                else:
                    got.append(in_2[o, dy].astype(F32)[:CAP])
        part = dot(gather, jnp.concatenate(got, axis=0).astype(BF16)).T
        for i, dz in enumerate(ORDER):
            low = max(OWNED * i, cols * st)
            high = min(OWNED * i + OWNED, cols * st + cols)
            if low >= high:
                continue
            value = part[low - cols * st : high - cols * st]
            if dz == 0:
                mine = value
                continue
            zx_out[dz, pl.ds(low - OWNED * i, high - low)] = value.astype(BF16)
            if high < OWNED * i + OWNED:
                continue
            copies[dz] = remote(
                zx_out.at[dz],
                zx_in.at[dz],
                zx_send.at[dz],
                zx_recv.at[dz],
                expert,
                (p + 4 * dz) % (4 * ZS),
            )
    work(len(tasks))
    for dz, copy in copies.items():
        copy.wait_recv()
        mine = mine + zx_in[dz].astype(F32)
    d_tokens_ref[...] = mine.astype(BF16)
    finish()


def hand_on(parts, t_ref, a_ref, b_ref, t_out, a_out, b_out, t_held, held, in_sem, out_sem):
    rows = a_ref.shape[1] // parts
    moves = [(t_ref, t_held, t_out, in_sem.at[0, parts], out_sem.at[0, parts])]
    for i in range(parts):
        at = pl.ds(i * rows, rows)
        for k, (src, dst) in enumerate(((a_ref, a_out), (b_ref, b_out))):
            moves.append(
                (src.at[0, at], held.at[k, at], dst.at[0, at], in_sem.at[k, i], out_sem.at[k, i])
            )
    loads = [pltpu.make_async_copy(src, mid, sem) for src, mid, _, sem, _ in moves]
    stores = [pltpu.make_async_copy(mid, dst, sem) for _, mid, dst, _, sem in moves]
    for load in loads:
        load.start()
    for load, store in zip(loads, stores):
        load.wait()
        store.start()
    for store in stores:
        store.wait()


def body(tokens, routes, w_gate, w_up, d_hidden):
    count, model_width = tokens.shape
    units = w_gate.shape[2]
    width = model_width // 4
    half = width // 2
    cols = width // STAGES
    dma = pltpu.SemaphoreType.DMA
    scratch = [
        pltpu.VMEM((2, count), jnp.int32),
        pltpu.VMEM((count, width), BF16),
        pltpu.VMEM((2 * count, units), BF16),
        pltpu.VMEM((2, 4, width, units), BF16),
        pltpu.VMEM((model_width, 2 * units), BF16),
        pltpu.VMEM((PARTS, EXPERTS, 2 * CAP, 128), BF16),
        pltpu.VMEM((4, PARTS, EXPERTS, 2 * CAP, 128), BF16),
        pltpu.VMEM((EXPERTS, 48, units), BF16),
        pltpu.VMEM((EXPERTS, 48, units), BF16),
        pltpu.VMEM((4, SLOTS, width), BF16),
        pltpu.VMEM((4, 2 * units, width), BF16),
        pltpu.VMEM((4, 2 * units, width), BF16),
        pltpu.VMEM((2, 2 * units, 2 * units), F32),
        pltpu.VMEM((2, 2 * units, 2 * units), BF16),
        pltpu.VMEM((2, width, 2 * units), BF16),
        pltpu.VMEM((2, width, 2 * units), BF16),
        pltpu.VMEM((2, width, 2 * units), BF16),
        pltpu.VMEM((SLOTS, 2 * units), BF16),
        pltpu.VMEM((SLOTS, 2 * units), BF16),
        pltpu.VMEM((EXPERTS, 2, CAP + 8, cols), BF16),
        pltpu.VMEM((EXPERTS, 2, CAP + 8, cols), BF16),
        pltpu.VMEM((EXPERTS, 2, CAP - 8, cols), BF16),
        pltpu.VMEM((EXPERTS, 2, CAP - 8, cols), BF16),
        pltpu.VMEM((EXPERTS, 2, CAP + 8, cols), BF16),
        pltpu.VMEM((EXPERTS, 2, CAP + 8, cols), BF16),
        pltpu.VMEM((ZS, 48, count), BF16),
        pltpu.VMEM((ZS, 48, count), BF16),
        pltpu.VMEM((EXPERTS, CAP, count), F32),
        pltpu.SemaphoreType.REGULAR((3,)),
        dma((5,)),
        dma((2, 4)),
    ]
    for shape in (
        (PARTS, EXPERTS),
        (EXPERTS,),
        (PARTS, len(GROUPS)),
        (PARTS, len(GROUPS)),
        (PARTS, len(GROUPS)),
        (2,),
        (STAGES, EXPERTS, 2),
        (ZS,),
    ):
        scratch += [dma(shape), dma(shape)]
    vmem = pl.BlockSpec(memory_space=pltpu.VMEM)
    anywhere = pl.BlockSpec(memory_space=pl.ANY)
    d_tokens, update_gate, update_up = pl.pallas_call(
        kernel,
        out_shape=(
            jax.ShapeDtypeStruct((48, count), BF16),
            jax.ShapeDtypeStruct(w_gate.shape, BF16),
            jax.ShapeDtypeStruct(w_up.shape, BF16),
        ),
        in_specs=[anywhere] * 5,
        out_specs=(vmem, anywhere, anywhere),
        scratch_shapes=scratch,
        compiler_params=pltpu.CompilerParams(
            collective_id=0, has_side_effects=True, vmem_limit_bytes=56 * 1024 * 1024
        ),
    )(tokens, routes.T, w_gate, w_up, d_hidden.reshape(2 * count, units))
    parts = 4
    d_tokens, update_gate, update_up = pl.pallas_call(
        functools.partial(hand_on, parts),
        out_shape=(
            jax.ShapeDtypeStruct((48, count), BF16),
            jax.ShapeDtypeStruct(w_gate.shape, BF16),
            jax.ShapeDtypeStruct(w_up.shape, BF16),
        ),
        in_specs=[anywhere] * 3,
        out_specs=(anywhere,) * 3,
        scratch_shapes=[
            pltpu.VMEM((48, count), BF16),
            pltpu.VMEM((2, model_width, units), BF16),
            dma((2, parts + 1)),
            dma((2, parts + 1)),
        ],
    )(d_tokens, update_gate, update_up)
    return d_tokens.T, update_gate, update_up


def solution(mesh):
    in_specs = (
        P("expert", None),
        P("expert", None),
        P("expert", None, "etp"),
        P("expert", None, "etp"),
        P("expert", None, "etp"),
    )
    out_specs = (P("expert", "etp"), P("expert", None, "etp"), P("expert", None, "etp"))
    return jax.shard_map(body, mesh=mesh, in_specs=in_specs, out_specs=out_specs, check_vma=False)
```

```python
import functools

import jax
import jax.numpy as jnp
from jax import lax
from jax.experimental import pallas as pl
from jax.experimental.pallas import tpu as pltpu
from jax.sharding import PartitionSpec as P

EXPERTS = 8
ZS = 16
BLK = 128
CAP = 40
SLOTS = EXPERTS * CAP
FAR_FIRST = (5, 3, 4, 7, 1, 6, 2)
PIECES = (256, 512, 512, 256)
ORDER = (8, 7, 9, 6, 10, 5, 11, 4, 12, 3, 13, 2, 14, 1, 15, 0)
STAGES = 3
OWNED = 48
WORK = (8, 2, 1)

NS_FIRST = 3.4445
NS_SECOND = -4.775
NS_THIRD = 2.0315

MESH = pl.DeviceIdType.MESH
F32 = jnp.float32
BF16 = jnp.bfloat16


def dot(a, b):
    return jnp.dot(a, b, preferred_element_type=F32)


def dot_nt(a, b):
    return lax.dot_general(a, b, (((1,), (1,)), ((), ())), preferred_element_type=F32)


def dot_exact(a, b):
    return jnp.dot(a, b, precision=lax.Precision.HIGHEST, preferred_element_type=F32)


def kernel(
    tokens_ref,
    routes_ref,
    w_gate_ref,
    w_up_ref,
    dh_ref,
    d_tokens_ref,
    update_gate_ref,
    update_up_ref,
    routes,
    tok,
    dh,
    updates,
    wcat,
    rows_out_0,
    rows_out_1,
    rows_out_2,
    land_0,
    land_1,
    land_2,
    land_3,
    cot_out,
    cot_land,
    srows,
    a_hi,
    a_lo,
    gram,
    mix,
    w_own,
    w_out,
    w_in,
    d_out,
    d_in,
    out_0,
    in_0,
    out_1,
    in_1,
    out_2,
    in_2,
    zx_out,
    zx_in,
    pmat,
    known,
    in_sem,
    out_sem,
    s1_send,
    s1_recv,
    cot_send,
    cot_recv,
    z_send,
    z_recv,
    c0_send,
    c0_recv,
    swap_send,
    swap_recv,
    a2a_send,
    a2a_recv,
    zx_send,
    zx_recv,
):
    rows_out = (rows_out_0, rows_out_1, rows_out_2)
    land = (land_0, land_1, land_2, land_3)
    expert = lax.axis_index("expert")
    p = lax.axis_index("etp")
    z = p // 4
    y = (p // 2) % 2
    core = p % 2
    width = wcat.shape[0] // 4

    def peer(o):
        return (expert + o) % EXPERTS

    def back_peer(o):
        return (expert + EXPERTS - o) % EXPERTS

    core_mate = z * 4 + y * 2 + (1 - core)
    y_mate = z * 4 + (1 - y) * 2 + core

    def near(e):
        cross = (expert + e) % 2
        return z * 4 + ((y + cross) % 2) * 2 + core

    z_to = (p + 4 * ZS + 4 - 8 * core) % (4 * ZS)

    def places_of(which):
        shared = 4 * PIECES[0]
        kept = shared + which * (PIECES[1] + PIECES[2])
        return (
            PIECES[0] * (2 * (z % 2) + which),
            kept,
            kept + PIECES[1],
            PIECES[0] * (2 * (1 - z % 2) + which),
        )

    starts = (places_of(core), places_of(1 - core))

    lanes = (0, PIECES[0], PIECES[0] + PIECES[1], 2 * width - PIECES[3])
    tok_copies = [
        pltpu.make_async_copy(
            tokens_ref.at[:, pl.ds(pl.multiple_of(starts[0][j], 128), PIECES[j])],
            tok.at[:, pl.ds(lanes[j], PIECES[j])],
            in_sem.at[(0, 5, 6)[j]],
        )
        for j in range(3)
    ]
    wg_copy = pltpu.make_async_copy(w_gate_ref.at[0], wcat.at[:, pl.ds(0, BLK)], in_sem.at[1])
    wu_copy = pltpu.make_async_copy(w_up_ref.at[0], wcat.at[:, pl.ds(BLK, BLK)], in_sem.at[2])
    dh_copy = pltpu.make_async_copy(dh_ref, dh, in_sem.at[3])
    routes_copy = pltpu.make_async_copy(routes_ref, routes, in_sem.at[4])
    routes_copy.start()
    for copy in tok_copies:
        copy.start()
    dh_copy.start()
    wg_copy.start()
    wu_copy.start()

    barrier = pltpu.get_barrier_semaphore()

    def greet(e, d):
        pl.semaphore_signal(
            barrier, inc=1, device_id={"expert": e, "etp": d}, device_id_type=MESH
        )

    for o in range(1, EXPERTS):
        greet(peer(o), p)
    for o in range(EXPERTS):
        greet(peer(o), y_mate)
    greet(expert, core_mate)
    for dz in (1, ZS - 1):
        greet(expert, (p + 4 * dz) % (4 * ZS))

    lane = lax.broadcasted_iota(jnp.int32, (128, 128), 1)
    row = lax.broadcasted_iota(jnp.int32, (128, 128), 0)
    routes_copy.wait()
    names_0 = jnp.where(row == routes[0:1, :], 1.0, 0.0)
    names_1 = jnp.where(row == routes[1:2, :], 1.0, 0.0)
    names = names_0 + names_1
    before = jnp.where(row < lane, 1.0, 0.0).astype(BF16)
    position = dot(names.astype(BF16), before)
    position = jnp.where(names > 0.5, position, -1.0)
    slot = row[:CAP].astype(F32)
    places = []
    for e in range(EXPERTS):
        place = jnp.where(slot == position[e : e + 1, :], 1.0, 0.0)
        pmat[e] = place
        places.append(place)
    for copy in tok_copies:
        copy.wait()
    placed = dot(jnp.concatenate(places, axis=0).astype(BF16), tok[...])
    for e in range(EXPERTS):
        rows = placed[CAP * e : CAP * e + CAP]
        for j in range(3):
            mid = lanes[j] + PIECES[j] // 2
            left, right = rows[:, lanes[j] : mid], rows[:, mid : lanes[j] + PIECES[j]]
            rows_out[j][e] = jnp.concatenate([left, right], axis=0).astype(BF16)

    pl.semaphore_wait(barrier, (EXPERTS - 1) + EXPERTS + 1 + 2)

    sends = []
    stores = []

    def finish():
        for copy in sends:
            copy.wait_send()
        for copy in stores:
            copy.wait()

    def remote(src, dst, send_sem, recv_sem, e, d):
        copy = pltpu.make_async_remote_copy(
            src_ref=src,
            dst_ref=dst,
            send_sem=send_sem,
            recv_sem=recv_sem,
            device_id={"expert": e, "etp": d},
            device_id_type=MESH,
        )
        copy.start()
        sends.append(copy)
        return copy

    def tell(step):
        for dz in (1 << step, ZS - (1 << step)):
            pl.semaphore_signal(
                known.at[step],
                inc=1,
                device_id={"expert": expert, "etp": (p + 4 * dz) % (4 * ZS)},
                device_id_type=MESH,
            )

    def hear(step):
        pl.semaphore_wait(known.at[step], 2)

    stage1 = {}
    for j in range(3):
        for o in range(1, EXPERTS):
            stage1[j, o] = remote(
                rows_out[j].at[peer(o)],
                land[j].at[0, o],
                s1_send.at[j, o],
                s1_recv.at[j, o],
                peer(o),
                near(peer(o)),
            )
    tell(0)
    first = [places[e] * names_0[e : e + 1, :] for e in range(EXPERTS)]
    second = [places[e] * names_1[e : e + 1, :] for e in range(EXPERTS)]
    token_of = lax.broadcasted_iota(jnp.int32, (128, 256), 0)
    choice = lax.broadcasted_iota(jnp.int32, (128, 256), 1)
    even = jnp.where(choice == 2 * token_of, 1.0, 0.0).astype(BF16)
    odd = jnp.where(choice == 2 * token_of + 1, 1.0, 0.0).astype(BF16)
    placing = dot(jnp.concatenate(first, axis=0).astype(BF16), even)
    placing = placing + dot(jnp.concatenate(second, axis=0).astype(BF16), odd)
    dh_copy.wait()
    cot = dot(placing.astype(BF16), dh[...])
    for e in range(EXPERTS):
        padded = jnp.concatenate(
            [cot[CAP * e : CAP * e + CAP], jnp.zeros((8, 128), F32)], axis=0
        )
        cot_out[e] = padded.astype(BF16)
    cots = {}
    for o in FAR_FIRST:
        cots[o] = remote(
            cot_out.at[peer(o)], cot_land.at[o], cot_send.at[o], cot_recv.at[o], peer(o), p
        )
    for j in range(3):
        land[j][0, 0] = rows_out[j][expert]
    cot_land[0] = cot_out[expert]
    gather = jnp.concatenate(
        [pmat[peer(o)] for o in range(EXPERTS) for _ in range(2)], axis=0
    ).T.astype(BF16)

    def compact(r, j):
        mid = PIECES[j] // 2
        lane_at = lanes[j] % width
        for i in range(EXPERTS // 2):
            one = land[j][r, 2 * i].astype(F32)
            two = land[j][r, 2 * i + 1].astype(F32)
            left = jnp.concatenate([one[:CAP], two[:CAP]], axis=0)
            right = jnp.concatenate([one[CAP:], two[CAP:]], axis=0)
            at = pl.ds(2 * CAP * i, 2 * CAP)
            srows[2 * r + j // 2, at, pl.ds(lane_at, mid)] = left.astype(BF16)
            srows[2 * r + j // 2, at, pl.ds(lane_at + mid, mid)] = right.astype(BF16)

    def forward(r, j):
        compact(r, j)
        at = pl.multiple_of(starts[r][j], 128)
        rows = srows[2 * r + j // 2, :, pl.ds(lanes[j] % width, PIECES[j])]
        return dot(rows, wcat[pl.ds(at, PIECES[j]), :])

    def sort_weights(out_ref, which):
        for side in range(2):
            for i, dz in enumerate(ORDER):
                at = ((z + dz) % ZS) * 192 + side * 96 + which * OWNED
                out_ref[side, pl.ds(OWNED * i, OWNED), :] = wcat[
                    pl.ds(pl.multiple_of(at, 16), OWNED), :
                ]

    wg_copy.wait()
    wu_copy.wait()
    sort_weights(w_out, 1 - core)
    w_swap = remote(w_out, w_in, swap_send.at[0], swap_recv.at[0], expert, core_mate)
    sort_weights(w_own, core)
    hear(0)
    tell(1)

    passed = []

    def pass_on(j):
        passed.append(
            remote(
                land[j].at[0], land[j].at[1], c0_send.at[j], c0_recv.at[j], expert, core_mate
            )
        )

    def arrived(j):
        for o in range(1, EXPERTS):
            stage1[j, o].wait_recv()

    arrived(0)
    along = remote(land[0].at[0], land[3].at[0], z_send.at[0], z_recv.at[0], expert, z_to)
    pass_on(0)
    acts = forward(0, 0)
    hear(1)
    tell(2)
    arrived(1)
    pass_on(1)
    along.wait_recv()
    pass_on(3)
    acts = acts + forward(0, 1)
    acts = acts + forward(0, 3)
    passed[0].wait_recv()
    acts = acts + forward(1, 0)
    arrived(2)
    pass_on(2)
    acts = acts + forward(0, 2)
    for o in FAR_FIRST:
        cots[o].wait_recv()
    cotangent = jnp.concatenate(
        [cot_land[o].astype(F32)[:CAP] for o in range(EXPERTS)], axis=0
    )
    for copy, j in zip(passed[1:], (1, 3, 2)):
        copy.wait_recv()
        acts = acts + forward(1, j)

    gate_act, up_act = acts[:, :BLK], acts[:, BLK:]
    sig = jax.nn.sigmoid(gate_act)
    d_up = cotangent * gate_act * sig
    d_gate = cotangent * up_act * sig * (1.0 + gate_act * (1.0 - sig))
    d_both = jnp.concatenate([d_gate, d_up], axis=1)
    d_rows = d_both.astype(BF16)
    d_out[...] = d_rows
    d_swap = remote(d_out, d_in, swap_send.at[1], swap_recv.at[1], expert, core_mate)
    d_both = jnp.concatenate([d_both, jnp.zeros((384 - SLOTS, 2 * BLK), F32)], axis=0)
    d_t = d_both.T.astype(BF16)[:, :SLOTS]

    def grad_piece(r):
        grad = dot(d_t, srows[r])
        hi = grad.astype(BF16)
        lo = (grad - hi.astype(F32)).astype(BF16)
        a_hi[r] = hi
        a_lo[r] = lo
        if r == 0:
            gram[0] = dot_nt(hi, hi)
            gram[1] = dot_nt(hi, lo)
        else:
            gram[0] = gram[0] + dot_nt(hi, hi)
            gram[1] = gram[1] + dot_nt(hi, lo)

    wide_row = lax.broadcasted_iota(jnp.int32, (256, 256), 0)
    wide_lane = lax.broadcasted_iota(jnp.int32, (256, 256), 1)
    state = {}

    def ns_start():
        cross = gram[1]
        g = gram[0] + cross + cross.T
        g = jnp.where((wide_row < BLK) == (wide_lane < BLK), g, 0.0)
        diagonal = jnp.where(wide_row == wide_lane, g, 0.0)
        sum_gate = jnp.sum(diagonal[:BLK], keepdims=True)
        sum_up = jnp.sum(diagonal[BLK:], keepdims=True)
        scale = jnp.where(
            wide_row < BLK, lax.rsqrt(sum_gate + 1e-06), lax.rsqrt(sum_up + 1e-06)
        )
        state["scale"] = scale
        state["g"] = g * scale * scale

    def polynomial(g):
        square = dot_exact(g, g)
        return jnp.where(wide_row == wide_lane, NS_FIRST, 0.0) + NS_SECOND * g + NS_THIRD * square

    def ns_one():
        g = state["g"]
        poly = polynomial(g)
        state["m"] = poly
        state["g"] = dot_exact(dot_exact(g, poly), poly)

    def ns_two():
        g = state["g"]
        poly = polynomial(g)
        both = dot_exact(jnp.concatenate([state["m"], g], axis=0), poly)
        state["m"] = both[:256]
        state["g"] = dot_exact(both[256:], poly)

    def ns_three():
        m = dot_exact(state["m"], polynomial(state["g"])) * state["scale"]
        hi = m.astype(BF16)
        mix[0] = hi
        mix[1] = (m - hi.astype(F32)).astype(BF16)

    def update_piece(r):
        hi = a_hi[r]
        update = dot(mix[0], hi) + dot(mix[1], hi) + dot(mix[0], a_lo[r])
        update = update.T.astype(BF16)
        low = 0
        for i, j in enumerate((2 * (r % 2), 2 * (r % 2) + 1)):
            at = pl.ds(pl.multiple_of(starts[r // 2][j], 128), PIECES[j])
            here = pl.ds(low, PIECES[j])
            for k, out_ref in enumerate((update_gate_ref, update_up_ref)):
                updates[k, r, here] = update[low : low + PIECES[j], BLK * k : BLK * k + BLK]
                copy = pltpu.make_async_copy(
                    updates.at[k, r, here], out_ref.at[0, at], out_sem.at[k, r, i]
                )
                copy.start()
                stores.append(copy)
            low += PIECES[j]

    tasks = [functools.partial(grad_piece, r) for r in range(4)]
    tasks += [ns_start, ns_one, ns_two, ns_three]
    tasks += [functools.partial(update_piece, r) for r in range(4)]

    def work(count):
        for _ in range(count):
            if tasks:
                tasks.pop(0)()

    cols = width // STAGES

    def back(rows, weights, st):
        at = pl.ds(cols * st, cols)
        return dot_nt(rows, jnp.concatenate([weights[0, at], weights[1, at]], axis=0))

    totals = [back(d_rows, w_own, st) for st in range(STAGES)]
    w_swap.wait_recv()
    d_swap.wait_recv()
    d_mate = d_in[...]

    returns = {}
    for st in range(STAGES):
        for more in {0: (0, 1), 1: (), 2: (2,)}[st]:
            totals[more] = totals[more] + back(d_mate, w_in, more)
        out_ref, in_ref = ((out_0, in_0), (out_1, in_1), (out_2, in_2))[st]
        for o in FAR_FIRST + (0,):
            low, high = CAP * o, CAP * o + CAP
            for side in range(2):
                cut = slice(cols * side, cols * side + cols)
                if st == 0:
                    block = [totals[0][low:high, cut], totals[1][high - 8 : high, cut]]
                elif st == 1:
                    block = [totals[1][low : high - 8, cut]]
                else:
                    block = [totals[2][low:high, cut], jnp.zeros((8, cols), F32)]
                out_ref[o, side] = jnp.concatenate(block, axis=0).astype(BF16)
            for dy in (1, 0):
                to_y = (y + dy) % 2
                if o == 0 and dy == 0:
                    in_ref[0, 0] = out_ref[0, y]
                    continue
                returns[st, o, dy] = remote(
                    out_ref.at[o, to_y],
                    in_ref.at[o, dy],
                    a2a_send.at[st, o, dy],
                    a2a_recv.at[st, o, dy],
                    back_peer(o),
                    z * 4 + to_y * 2 + core,
                )
    hear(2)
    copies = {}
    for st in range(STAGES):
        work(WORK[st])
        got = []
        for o in range(EXPERTS):
            for dy in range(2):
                if (st, o, dy) in returns:
                    returns[st, o, dy].wait_recv()
                if st == 0:
                    got.append(in_0[o, dy].astype(F32)[:CAP])
                elif st == 1:
                    got.append(in_1[o, dy].astype(F32))
                    got.append(in_0[o, dy].astype(F32)[CAP:])
                else:
                    got.append(in_2[o, dy].astype(F32)[:CAP])
        part = dot(gather, jnp.concatenate(got, axis=0).astype(BF16)).T
        for i, dz in enumerate(ORDER):
            low = max(OWNED * i, cols * st)
            high = min(OWNED * i + OWNED, cols * st + cols)
            if low >= high:
                continue
            value = part[low - cols * st : high - cols * st]
            if dz == 0:
                mine = value
                continue
            zx_out[dz, pl.ds(low - OWNED * i, high - low)] = value.astype(BF16)
            if high < OWNED * i + OWNED:
                continue
            copies[dz] = remote(
                zx_out.at[dz],
                zx_in.at[dz],
                zx_send.at[dz],
                zx_recv.at[dz],
                expert,
                (p + 4 * dz) % (4 * ZS),
            )
    work(len(tasks))
    for dz, copy in copies.items():
        copy.wait_recv()
        mine = mine + zx_in[dz].astype(F32)
    d_tokens_ref[...] = mine.astype(BF16)
    finish()


def hand_on(parts, t_ref, a_ref, b_ref, t_out, a_out, b_out, t_held, held, in_sem, out_sem):
    rows = a_ref.shape[1] // parts
    moves = [(t_ref, t_held, t_out, in_sem.at[0, parts], out_sem.at[0, parts])]
    for i in range(parts):
        at = pl.ds(i * rows, rows)
        for k, (src, dst) in enumerate(((a_ref, a_out), (b_ref, b_out))):
            moves.append(
                (src.at[0, at], held.at[k, at], dst.at[0, at], in_sem.at[k, i], out_sem.at[k, i])
            )
    loads = [pltpu.make_async_copy(src, mid, sem) for src, mid, _, sem, _ in moves]
    stores = [pltpu.make_async_copy(mid, dst, sem) for _, mid, dst, _, sem in moves]
    for load in loads:
        load.start()
    for load, store in zip(loads, stores):
        load.wait()
        store.start()
    for store in stores:
        store.wait()


def body(tokens, routes, w_gate, w_up, d_hidden):
    count, model_width = tokens.shape
    units = w_gate.shape[2]
    width = model_width // 4
    half = width // 2
    cols = width // STAGES
    dma = pltpu.SemaphoreType.DMA
    scratch = [
        pltpu.VMEM((2, count), jnp.int32),
        pltpu.VMEM((count, 2 * width - PIECES[3]), BF16),
        pltpu.VMEM((2 * count, units), BF16),
        pltpu.VMEM((2, 4, width, units), BF16),
        pltpu.VMEM((model_width, 2 * units), BF16),
        *[pltpu.VMEM((EXPERTS, 2 * CAP, PIECES[j] // 2), BF16) for j in range(3)],
        *[pltpu.VMEM((2, EXPERTS, 2 * CAP, PIECES[j] // 2), BF16) for j in range(4)],
        pltpu.VMEM((EXPERTS, 48, units), BF16),
        pltpu.VMEM((EXPERTS, 48, units), BF16),
        pltpu.VMEM((4, SLOTS, width), BF16),
        pltpu.VMEM((4, 2 * units, width), BF16),
        pltpu.VMEM((4, 2 * units, width), BF16),
        pltpu.VMEM((2, 2 * units, 2 * units), F32),
        pltpu.VMEM((2, 2 * units, 2 * units), BF16),
        pltpu.VMEM((2, width, 2 * units), BF16),
        pltpu.VMEM((2, width, 2 * units), BF16),
        pltpu.VMEM((2, width, 2 * units), BF16),
        pltpu.VMEM((SLOTS, 2 * units), BF16),
        pltpu.VMEM((SLOTS, 2 * units), BF16),
        pltpu.VMEM((EXPERTS, 2, CAP + 8, cols), BF16),
        pltpu.VMEM((EXPERTS, 2, CAP + 8, cols), BF16),
        pltpu.VMEM((EXPERTS, 2, CAP - 8, cols), BF16),
        pltpu.VMEM((EXPERTS, 2, CAP - 8, cols), BF16),
        pltpu.VMEM((EXPERTS, 2, CAP + 8, cols), BF16),
        pltpu.VMEM((EXPERTS, 2, CAP + 8, cols), BF16),
        pltpu.VMEM((ZS, 48, count), BF16),
        pltpu.VMEM((ZS, 48, count), BF16),
        pltpu.VMEM((EXPERTS, CAP, count), F32),
        pltpu.SemaphoreType.REGULAR((3,)),
        dma((7,)),
        dma((2, 4, 2)),
    ]
    for shape in (
        (3, EXPERTS),
        (EXPERTS,),
        (1,),
        (4,),
        (2,),
        (STAGES, EXPERTS, 2),
        (ZS,),
    ):
        scratch += [dma(shape), dma(shape)]
    vmem = pl.BlockSpec(memory_space=pltpu.VMEM)
    anywhere = pl.BlockSpec(memory_space=pl.ANY)
    d_tokens, update_gate, update_up = pl.pallas_call(
        kernel,
        out_shape=(
            jax.ShapeDtypeStruct((48, count), BF16),
            jax.ShapeDtypeStruct(w_gate.shape, BF16),
            jax.ShapeDtypeStruct(w_up.shape, BF16),
        ),
        in_specs=[anywhere] * 5,
        out_specs=(vmem, anywhere, anywhere),
        scratch_shapes=scratch,
        compiler_params=pltpu.CompilerParams(
            collective_id=0, has_side_effects=True, vmem_limit_bytes=56 * 1024 * 1024
        ),
    )(tokens, routes.T, w_gate, w_up, d_hidden.reshape(2 * count, units))
    parts = 4
    d_tokens, update_gate, update_up = pl.pallas_call(
        functools.partial(hand_on, parts),
        out_shape=(
            jax.ShapeDtypeStruct((48, count), BF16),
            jax.ShapeDtypeStruct(w_gate.shape, BF16),
            jax.ShapeDtypeStruct(w_up.shape, BF16),
        ),
        in_specs=[anywhere] * 3,
        out_specs=(anywhere,) * 3,
        scratch_shapes=[
            pltpu.VMEM((48, count), BF16),
            pltpu.VMEM((2, model_width, units), BF16),
            dma((2, parts + 1)),
            dma((2, parts + 1)),
        ],
    )(d_tokens, update_gate, update_up)
    return d_tokens.T, update_gate, update_up


def solution(mesh):
    in_specs = (
        P("expert", None),
        P("expert", None),
        P("expert", None, "etp"),
        P("expert", None, "etp"),
        P("expert", None, "etp"),
    )
    out_specs = (P("expert", "etp"), P("expert", None, "etp"), P("expert", None, "etp"))
    return jax.shard_map(body, mesh=mesh, in_specs=in_specs, out_specs=out_specs, check_vma=False)
```

```python
import functools

import jax
import jax.numpy as jnp
from jax import lax
from jax.experimental import pallas as pl
from jax.experimental.pallas import tpu as pltpu
from jax.sharding import PartitionSpec as P

EXPERTS = 8
ZS = 16
BLK = 128
CAP = 40
SLOTS = EXPERTS * CAP
FAR_FIRST = (5, 3, 4, 7, 1, 6, 2)
PIECES = (256, 512, 512, 256)
ORDER = (8, 7, 9, 6, 10, 5, 11, 4, 12, 3, 13, 2, 14, 1, 15, 0)
STAGES = 3
OWNED = 48
WORK = (8, 2, 1)

NS_FIRST = 3.4445
NS_SECOND = -4.775
NS_THIRD = 2.0315

MESH = pl.DeviceIdType.MESH
F32 = jnp.float32
BF16 = jnp.bfloat16


def dot(a, b):
    return jnp.dot(a, b, preferred_element_type=F32)


def dot_nt(a, b):
    return lax.dot_general(a, b, (((1,), (1,)), ((), ())), preferred_element_type=F32)


def dot_exact(a, b):
    return jnp.dot(a, b, precision=lax.Precision.HIGHEST, preferred_element_type=F32)


def kernel(
    tokens_ref,
    routes_ref,
    w_gate_ref,
    w_up_ref,
    dh_ref,
    d_tokens_ref,
    update_gate_ref,
    update_up_ref,
    routes,
    tok,
    dh,
    updates,
    wcat,
    rows_out_0,
    rows_out_1,
    rows_out_2,
    land_0,
    land_1,
    land_2,
    land_3,
    cot_out,
    cot_land,
    srows,
    a_hi,
    a_lo,
    gram,
    mix,
    w_own,
    w_out,
    w_in,
    d_out,
    d_in,
    sums_out,
    sums_in,
    zx_out,
    zx_in,
    pmat,
    known,
    in_sem,
    out_sem,
    s1_send,
    s1_recv,
    cot_send,
    cot_recv,
    z_send,
    z_recv,
    c0_send,
    c0_recv,
    swap_send,
    swap_recv,
    a2a_send,
    a2a_recv,
    zx_send,
    zx_recv,
):
    rows_out = (rows_out_0, rows_out_1, rows_out_2)
    land = (land_0, land_1, land_2, land_3)
    expert = lax.axis_index("expert")
    p = lax.axis_index("etp")
    z = p // 4
    y = (p // 2) % 2
    core = p % 2
    width = wcat.shape[0] // 4

    def peer(o):
        return (expert + o) % EXPERTS

    def back_peer(o):
        return (expert + EXPERTS - o) % EXPERTS

    core_mate = z * 4 + y * 2 + (1 - core)
    y_mate = z * 4 + (1 - y) * 2 + core

    def near(e):
        cross = (expert + e) % 2
        return z * 4 + ((y + cross) % 2) * 2 + core

    z_to = (p + 4 * ZS + 4 - 8 * core) % (4 * ZS)

    def places_of(which):
        shared = 4 * PIECES[0]
        kept = shared + which * (PIECES[1] + PIECES[2])
        return (
            PIECES[0] * (2 * (z % 2) + which),
            kept,
            kept + PIECES[1],
            PIECES[0] * (2 * (1 - z % 2) + which),
        )

    starts = (places_of(core), places_of(1 - core))

    lanes = (0, PIECES[0], PIECES[0] + PIECES[1], 2 * width - PIECES[3])
    tok_copies = [
        pltpu.make_async_copy(
            tokens_ref.at[:, pl.ds(pl.multiple_of(starts[0][j], 128), PIECES[j])],
            tok.at[:, pl.ds(lanes[j], PIECES[j])],
            in_sem.at[(0, 5, 6)[j]],
        )
        for j in range(3)
    ]
    wg_copy = pltpu.make_async_copy(w_gate_ref.at[0], wcat.at[:, pl.ds(0, BLK)], in_sem.at[1])
    wu_copy = pltpu.make_async_copy(w_up_ref.at[0], wcat.at[:, pl.ds(BLK, BLK)], in_sem.at[2])
    dh_copy = pltpu.make_async_copy(dh_ref, dh, in_sem.at[3])
    routes_copy = pltpu.make_async_copy(routes_ref, routes, in_sem.at[4])
    routes_copy.start()
    for copy in tok_copies:
        copy.start()
    dh_copy.start()
    wg_copy.start()
    wu_copy.start()

    barrier = pltpu.get_barrier_semaphore()

    def greet(e, d):
        pl.semaphore_signal(
            barrier, inc=1, device_id={"expert": e, "etp": d}, device_id_type=MESH
        )

    for o in range(1, EXPERTS):
        greet(peer(o), p)
    for o in range(EXPERTS):
        greet(peer(o), y_mate)
    greet(expert, core_mate)
    for dz in (1, ZS - 1):
        greet(expert, (p + 4 * dz) % (4 * ZS))

    lane = lax.broadcasted_iota(jnp.int32, (128, 128), 1)
    row = lax.broadcasted_iota(jnp.int32, (128, 128), 0)
    routes_copy.wait()
    names_0 = jnp.where(row == routes[0:1, :], 1.0, 0.0)
    names_1 = jnp.where(row == routes[1:2, :], 1.0, 0.0)
    names = names_0 + names_1
    before = jnp.where(row < lane, 1.0, 0.0).astype(BF16)
    position = dot(names.astype(BF16), before)
    position = jnp.where(names > 0.5, position, -1.0)
    slot = row[:CAP].astype(F32)
    places = []
    for e in range(EXPERTS):
        place = jnp.where(slot == position[e : e + 1, :], 1.0, 0.0)
        pmat[e] = place
        places.append(place)
    for copy in tok_copies:
        copy.wait()
    placed = dot(jnp.concatenate(places, axis=0).astype(BF16), tok[...])
    for e in range(EXPERTS):
        rows = placed[CAP * e : CAP * e + CAP]
        for j in range(3):
            mid = lanes[j] + PIECES[j] // 2
            left, right = rows[:, lanes[j] : mid], rows[:, mid : lanes[j] + PIECES[j]]
            rows_out[j][e] = jnp.concatenate([left, right], axis=0).astype(BF16)

    pl.semaphore_wait(barrier, (EXPERTS - 1) + EXPERTS + 1 + 2)

    sends = []
    stores = []

    def finish():
        for copy in sends:
            copy.wait_send()
        for copy in stores:
            copy.wait()

    def remote(src, dst, send_sem, recv_sem, e, d):
        copy = pltpu.make_async_remote_copy(
            src_ref=src,
            dst_ref=dst,
            send_sem=send_sem,
            recv_sem=recv_sem,
            device_id={"expert": e, "etp": d},
            device_id_type=MESH,
        )
        copy.start()
        sends.append(copy)
        return copy

    def tell(step):
        for dz in (1 << step, ZS - (1 << step)):
            pl.semaphore_signal(
                known.at[step],
                inc=1,
                device_id={"expert": expert, "etp": (p + 4 * dz) % (4 * ZS)},
                device_id_type=MESH,
            )

    def hear(step):
        pl.semaphore_wait(known.at[step], 2)

    stage1 = {}
    for j in range(3):
        for o in range(1, EXPERTS):
            stage1[j, o] = remote(
                rows_out[j].at[peer(o)],
                land[j].at[0, o],
                s1_send.at[j, o],
                s1_recv.at[j, o],
                peer(o),
                near(peer(o)),
            )
    tell(0)
    first = [places[e] * names_0[e : e + 1, :] for e in range(EXPERTS)]
    second = [places[e] * names_1[e : e + 1, :] for e in range(EXPERTS)]
    token_of = lax.broadcasted_iota(jnp.int32, (128, 256), 0)
    choice = lax.broadcasted_iota(jnp.int32, (128, 256), 1)
    even = jnp.where(choice == 2 * token_of, 1.0, 0.0).astype(BF16)
    odd = jnp.where(choice == 2 * token_of + 1, 1.0, 0.0).astype(BF16)
    placing = dot(jnp.concatenate(first, axis=0).astype(BF16), even)
    placing = placing + dot(jnp.concatenate(second, axis=0).astype(BF16), odd)
    dh_copy.wait()
    cot = dot(placing.astype(BF16), dh[...])
    for e in range(EXPERTS):
        padded = jnp.concatenate(
            [cot[CAP * e : CAP * e + CAP], jnp.zeros((8, 128), F32)], axis=0
        )
        cot_out[e] = padded.astype(BF16)
    cots = {}
    for o in FAR_FIRST:
        cots[o] = remote(
            cot_out.at[peer(o)], cot_land.at[o], cot_send.at[o], cot_recv.at[o], peer(o), p
        )
    for j in range(3):
        land[j][0, 0] = rows_out[j][expert]
    cot_land[0] = cot_out[expert]
    gather = jnp.concatenate(
        [pmat[peer(o)] for o in range(EXPERTS) for _ in range(2)], axis=0
    ).T.astype(BF16)

    def compact(r, j):
        mid = PIECES[j] // 2
        lane_at = lanes[j] % width
        for i in range(EXPERTS // 2):
            one = land[j][r, 2 * i].astype(F32)
            two = land[j][r, 2 * i + 1].astype(F32)
            left = jnp.concatenate([one[:CAP], two[:CAP]], axis=0)
            right = jnp.concatenate([one[CAP:], two[CAP:]], axis=0)
            at = pl.ds(2 * CAP * i, 2 * CAP)
            srows[2 * r + j // 2, at, pl.ds(lane_at, mid)] = left.astype(BF16)
            srows[2 * r + j // 2, at, pl.ds(lane_at + mid, mid)] = right.astype(BF16)

    def forward(r, j):
        compact(r, j)
        at = pl.multiple_of(starts[r][j], 128)
        rows = srows[2 * r + j // 2, :, pl.ds(lanes[j] % width, PIECES[j])]
        return dot(rows, wcat[pl.ds(at, PIECES[j]), :])

    def sort_weights(out_ref, which):
        for side in range(2):
            for i, dz in enumerate(ORDER):
                at = ((z + dz) % ZS) * 192 + side * 96 + which * OWNED
                out_ref[side, pl.ds(OWNED * i, OWNED), :] = wcat[
                    pl.ds(pl.multiple_of(at, 16), OWNED), :
                ]

    wg_copy.wait()
    wu_copy.wait()
    sort_weights(w_out, 1 - core)
    w_swap = remote(w_out, w_in, swap_send.at[0], swap_recv.at[0], expert, core_mate)
    sort_weights(w_own, core)
    hear(0)
    tell(1)

    passed = []

    def pass_on(j):
        passed.append(
            remote(
                land[j].at[0], land[j].at[1], c0_send.at[j], c0_recv.at[j], expert, core_mate
            )
        )

    def arrived(j):
        for o in range(1, EXPERTS):
            stage1[j, o].wait_recv()

    arrived(0)
    along = remote(land[0].at[0], land[3].at[0], z_send.at[0], z_recv.at[0], expert, z_to)
    pass_on(0)
    acts = forward(0, 0)
    hear(1)
    tell(2)
    arrived(1)
    pass_on(1)
    along.wait_recv()
    pass_on(3)
    acts = acts + forward(0, 1)
    acts = acts + forward(0, 3)
    passed[0].wait_recv()
    acts = acts + forward(1, 0)
    arrived(2)
    pass_on(2)
    acts = acts + forward(0, 2)
    for o in FAR_FIRST:
        cots[o].wait_recv()
    cotangent = jnp.concatenate(
        [cot_land[o].astype(F32)[:CAP] for o in range(EXPERTS)], axis=0
    )
    for copy, j in zip(passed[1:], (1, 3, 2)):
        copy.wait_recv()
        acts = acts + forward(1, j)

    gate_act, up_act = acts[:, :BLK], acts[:, BLK:]
    sig = jax.nn.sigmoid(gate_act)
    d_up = cotangent * gate_act * sig
    d_gate = cotangent * up_act * sig * (1.0 + gate_act * (1.0 - sig))
    d_both = jnp.concatenate([d_gate, d_up], axis=1)
    d_rows = d_both.astype(BF16)
    d_out[...] = d_rows
    d_swap = remote(d_out, d_in, swap_send.at[1], swap_recv.at[1], expert, core_mate)
    d_both = jnp.concatenate([d_both, jnp.zeros((384 - SLOTS, 2 * BLK), F32)], axis=0)
    d_t = d_both.T.astype(BF16)[:, :SLOTS]

    def grad_piece(r):
        grad = dot(d_t, srows[r])
        hi = grad.astype(BF16)
        lo = (grad - hi.astype(F32)).astype(BF16)
        a_hi[r] = hi
        a_lo[r] = lo
        if r == 0:
            gram[0] = dot_nt(hi, hi)
            gram[1] = dot_nt(hi, lo)
        else:
            gram[0] = gram[0] + dot_nt(hi, hi)
            gram[1] = gram[1] + dot_nt(hi, lo)

    wide_row = lax.broadcasted_iota(jnp.int32, (256, 256), 0)
    wide_lane = lax.broadcasted_iota(jnp.int32, (256, 256), 1)
    state = {}

    def ns_start():
        cross = gram[1]
        g = gram[0] + cross + cross.T
        g = jnp.where((wide_row < BLK) == (wide_lane < BLK), g, 0.0)
        diagonal = jnp.where(wide_row == wide_lane, g, 0.0)
        sum_gate = jnp.sum(diagonal[:BLK], keepdims=True)
        sum_up = jnp.sum(diagonal[BLK:], keepdims=True)
        scale = jnp.where(
            wide_row < BLK, lax.rsqrt(sum_gate + 1e-06), lax.rsqrt(sum_up + 1e-06)
        )
        state["scale"] = scale
        state["g"] = g * scale * scale

    def polynomial(g):
        square = dot_exact(g, g)
        return jnp.where(wide_row == wide_lane, NS_FIRST, 0.0) + NS_SECOND * g + NS_THIRD * square

    def ns_one():
        g = state["g"]
        poly = polynomial(g)
        state["m"] = poly
        state["g"] = dot_exact(dot_exact(g, poly), poly)

    def ns_two():
        g = state["g"]
        poly = polynomial(g)
        both = dot_exact(jnp.concatenate([state["m"], g], axis=0), poly)
        state["m"] = both[:256]
        state["g"] = dot_exact(both[256:], poly)

    def ns_three():
        m = dot_exact(state["m"], polynomial(state["g"])) * state["scale"]
        hi = m.astype(BF16)
        mix[0] = hi
        mix[1] = (m - hi.astype(F32)).astype(BF16)

    def update_piece(r):
        hi = a_hi[r]
        update = dot(mix[0], hi) + dot(mix[1], hi) + dot(mix[0], a_lo[r])
        update = update.T.astype(BF16)
        low = 0
        for i, j in enumerate((2 * (r % 2), 2 * (r % 2) + 1)):
            at = pl.ds(pl.multiple_of(starts[r // 2][j], 128), PIECES[j])
            here = pl.ds(low, PIECES[j])
            for k, out_ref in enumerate((update_gate_ref, update_up_ref)):
                updates[k, r, here] = update[low : low + PIECES[j], BLK * k : BLK * k + BLK]
                copy = pltpu.make_async_copy(
                    updates.at[k, r, here], out_ref.at[0, at], out_sem.at[k, r, i]
                )
                copy.start()
                stores.append(copy)
            low += PIECES[j]

    tasks = [functools.partial(grad_piece, r) for r in range(4)]
    tasks += [ns_start, ns_one, ns_two, ns_three]
    tasks += [functools.partial(update_piece, r) for r in range(4)]

    def work(count):
        for _ in range(count):
            if tasks:
                tasks.pop(0)()

    cols = width // STAGES

    def back(rows, weights, st):
        at = pl.ds(cols * st, cols)
        return dot_nt(rows, jnp.concatenate([weights[0, at], weights[1, at]], axis=0))

    totals = [back(d_rows, w_own, st) for st in range(STAGES)]
    w_swap.wait_recv()
    d_swap.wait_recv()
    d_mate = d_in[...]

    returns = {}
    for st in range(STAGES):
        totals[st] = totals[st] + back(d_mate, w_in, st)
        out_ref, in_ref = sums_out.at[st], sums_in.at[st]
        for o in FAR_FIRST + (0,):
            low, high = CAP * o, CAP * o + CAP
            for side in range(2):
                block = [
                    totals[st][low:high, at : at + cols // 2]
                    for at in (cols * side, cols * side + cols // 2)
                ]
                out_ref[o, side] = jnp.concatenate(block, axis=0).astype(BF16)
            for dy in (1, 0):
                to_y = (y + dy) % 2
                if o == 0 and dy == 0:
                    in_ref[0, 0] = out_ref[0, y]
                    continue
                returns[st, o, dy] = remote(
                    out_ref.at[o, to_y],
                    in_ref.at[o, dy],
                    a2a_send.at[st, o, dy],
                    a2a_recv.at[st, o, dy],
                    back_peer(o),
                    z * 4 + to_y * 2 + core,
                )
    hear(2)
    copies = {}
    for st in range(STAGES):
        work(WORK[st])
        left, right = [], []
        for o in range(EXPERTS):
            for dy in range(2):
                if (st, o, dy) in returns:
                    returns[st, o, dy].wait_recv()
                block = sums_in[st, o, dy].astype(F32)
                left.append(block[:CAP])
                right.append(block[CAP:])
        got = [jnp.concatenate(left, axis=0), jnp.concatenate(right, axis=0)]
        part = dot(gather, jnp.concatenate(got, axis=1).astype(BF16)).T
        for i, dz in enumerate(ORDER):
            low = max(OWNED * i, cols * st)
            high = min(OWNED * i + OWNED, cols * st + cols)
            if low >= high:
                continue
            value = part[low - cols * st : high - cols * st]
            if dz == 0:
                mine = value
                continue
            zx_out[dz, pl.ds(low - OWNED * i, high - low)] = value.astype(BF16)
            if high < OWNED * i + OWNED:
                continue
            copies[dz] = remote(
                zx_out.at[dz],
                zx_in.at[dz],
                zx_send.at[dz],
                zx_recv.at[dz],
                expert,
                (p + 4 * dz) % (4 * ZS),
            )
    work(len(tasks))
    for dz, copy in copies.items():
        copy.wait_recv()
        mine = mine + zx_in[dz].astype(F32)
    d_tokens_ref[...] = mine.astype(BF16)
    finish()


def hand_on(parts, t_ref, a_ref, b_ref, t_out, a_out, b_out, t_held, held, in_sem, out_sem):
    rows = a_ref.shape[1] // parts
    moves = [(t_ref, t_held, t_out, in_sem.at[0, parts], out_sem.at[0, parts])]
    for i in range(parts):
        at = pl.ds(i * rows, rows)
        for k, (src, dst) in enumerate(((a_ref, a_out), (b_ref, b_out))):
            moves.append(
                (src.at[0, at], held.at[k, at], dst.at[0, at], in_sem.at[k, i], out_sem.at[k, i])
            )
    loads = [pltpu.make_async_copy(src, mid, sem) for src, mid, _, sem, _ in moves]
    stores = [pltpu.make_async_copy(mid, dst, sem) for _, mid, dst, _, sem in moves]
    for load in loads:
        load.start()
    for load, store in zip(loads, stores):
        load.wait()
        store.start()
    for store in stores:
        store.wait()


def body(tokens, routes, w_gate, w_up, d_hidden):
    count, model_width = tokens.shape
    units = w_gate.shape[2]
    width = model_width // 4
    half = width // 2
    cols = width // STAGES
    dma = pltpu.SemaphoreType.DMA
    scratch = [
        pltpu.VMEM((2, count), jnp.int32),
        pltpu.VMEM((count, 2 * width - PIECES[3]), BF16),
        pltpu.VMEM((2 * count, units), BF16),
        pltpu.VMEM((2, 4, width, units), BF16),
        pltpu.VMEM((model_width, 2 * units), BF16),
        *[pltpu.VMEM((EXPERTS, 2 * CAP, PIECES[j] // 2), BF16) for j in range(3)],
        *[pltpu.VMEM((2, EXPERTS, 2 * CAP, PIECES[j] // 2), BF16) for j in range(4)],
        pltpu.VMEM((EXPERTS, 48, units), BF16),
        pltpu.VMEM((EXPERTS, 48, units), BF16),
        pltpu.VMEM((4, SLOTS, width), BF16),
        pltpu.VMEM((4, 2 * units, width), BF16),
        pltpu.VMEM((4, 2 * units, width), BF16),
        pltpu.VMEM((2, 2 * units, 2 * units), F32),
        pltpu.VMEM((2, 2 * units, 2 * units), BF16),
        pltpu.VMEM((2, width, 2 * units), BF16),
        pltpu.VMEM((2, width, 2 * units), BF16),
        pltpu.VMEM((2, width, 2 * units), BF16),
        pltpu.VMEM((SLOTS, 2 * units), BF16),
        pltpu.VMEM((SLOTS, 2 * units), BF16),
        pltpu.VMEM((STAGES, EXPERTS, 2, 2 * CAP, cols // 2), BF16),
        pltpu.VMEM((STAGES, EXPERTS, 2, 2 * CAP, cols // 2), BF16),
        pltpu.VMEM((ZS, 48, count), BF16),
        pltpu.VMEM((ZS, 48, count), BF16),
        pltpu.VMEM((EXPERTS, CAP, count), F32),
        pltpu.SemaphoreType.REGULAR((3,)),
        dma((7,)),
        dma((2, 4, 2)),
    ]
    for shape in (
        (3, EXPERTS),
        (EXPERTS,),
        (1,),
        (4,),
        (2,),
        (STAGES, EXPERTS, 2),
        (ZS,),
    ):
        scratch += [dma(shape), dma(shape)]
    vmem = pl.BlockSpec(memory_space=pltpu.VMEM)
    anywhere = pl.BlockSpec(memory_space=pl.ANY)
    d_tokens, update_gate, update_up = pl.pallas_call(
        kernel,
        out_shape=(
            jax.ShapeDtypeStruct((48, count), BF16),
            jax.ShapeDtypeStruct(w_gate.shape, BF16),
            jax.ShapeDtypeStruct(w_up.shape, BF16),
        ),
        in_specs=[anywhere] * 5,
        out_specs=(vmem, anywhere, anywhere),
        scratch_shapes=scratch,
        compiler_params=pltpu.CompilerParams(
            collective_id=0, has_side_effects=True, vmem_limit_bytes=56 * 1024 * 1024
        ),
    )(tokens, routes.T, w_gate, w_up, d_hidden.reshape(2 * count, units))
    parts = 4
    d_tokens, update_gate, update_up = pl.pallas_call(
        functools.partial(hand_on, parts),
        out_shape=(
            jax.ShapeDtypeStruct((48, count), BF16),
            jax.ShapeDtypeStruct(w_gate.shape, BF16),
            jax.ShapeDtypeStruct(w_up.shape, BF16),
        ),
        in_specs=[anywhere] * 3,
        out_specs=(anywhere,) * 3,
        scratch_shapes=[
            pltpu.VMEM((48, count), BF16),
            pltpu.VMEM((2, model_width, units), BF16),
            dma((2, parts + 1)),
            dma((2, parts + 1)),
        ],
    )(d_tokens, update_gate, update_up)
    return d_tokens.T, update_gate, update_up


def solution(mesh):
    in_specs = (
        P("expert", None),
        P("expert", None),
        P("expert", None, "etp"),
        P("expert", None, "etp"),
        P("expert", None, "etp"),
    )
    out_specs = (P("expert", "etp"), P("expert", None, "etp"), P("expert", None, "etp"))
    return jax.shard_map(body, mesh=mesh, in_specs=in_specs, out_specs=out_specs, check_vma=False)
```

```python
import functools

import jax
import jax.numpy as jnp
from jax import lax
from jax.experimental import pallas as pl
from jax.experimental.pallas import tpu as pltpu
from jax.sharding import PartitionSpec as P

EXPERTS = 8
ZS = 16
BLK = 128
CAP = 40
SLOTS = EXPERTS * CAP
FAR_FIRST = (5, 3, 4, 7, 1, 6, 2)
PIECES = (256, 512, 512, 256)
ORDER = (8, 7, 9, 6, 10, 5, 11, 4, 12, 3, 13, 2, 14, 1, 15, 0)
STAGES = 3
OWNED = 48
WORK = (8, 2, 1)

NS_FIRST = 3.4445
NS_SECOND = -4.775
NS_THIRD = 2.0315

MESH = pl.DeviceIdType.MESH
F32 = jnp.float32
BF16 = jnp.bfloat16


def dot(a, b):
    return jnp.dot(a, b, preferred_element_type=F32)


def dot_nt(a, b):
    return lax.dot_general(a, b, (((1,), (1,)), ((), ())), preferred_element_type=F32)


def dot_exact(a, b):
    return jnp.dot(a, b, precision=lax.Precision.HIGHEST, preferred_element_type=F32)


def kernel(
    tokens_ref,
    routes_ref,
    w_gate_ref,
    w_up_ref,
    dh_ref,
    d_tokens_ref,
    update_gate_ref,
    update_up_ref,
    routes,
    tok,
    dh,
    updates,
    wcat,
    rows_out_0,
    rows_out_1,
    rows_out_2,
    land_0,
    land_1,
    land_2,
    land_3,
    cot_out,
    cot_land,
    srows,
    a_hi,
    a_lo,
    gram,
    mix,
    w_own,
    w_out,
    w_in,
    d_out,
    d_in,
    sums_out,
    sums_in,
    zx_out,
    zx_in,
    pmat,
    known,
    in_sem,
    out_sem,
    s1_send,
    s1_recv,
    cot_send,
    cot_recv,
    z_send,
    z_recv,
    c0_send,
    c0_recv,
    swap_send,
    swap_recv,
    a2a_send,
    a2a_recv,
    zx_send,
    zx_recv,
):
    rows_out = (rows_out_0, rows_out_1, rows_out_2)
    land = (land_0, land_1, land_2, land_3)
    expert = lax.axis_index("expert")
    p = lax.axis_index("etp")
    z = p // 4
    y = (p // 2) % 2
    core = p % 2
    width = wcat.shape[0] // 4

    def peer(o):
        return (expert + o) % EXPERTS

    def back_peer(o):
        return (expert + EXPERTS - o) % EXPERTS

    core_mate = z * 4 + y * 2 + (1 - core)
    y_mate = z * 4 + (1 - y) * 2 + core

    def near(e):
        cross = (expert + e) % 2
        return z * 4 + ((y + cross) % 2) * 2 + core

    z_to = (p + 4 * ZS + 4 - 8 * core) % (4 * ZS)

    def places_of(which):
        shared = 4 * PIECES[0]
        kept = shared + which * (PIECES[1] + PIECES[2])
        return (
            PIECES[0] * (2 * (z % 2) + which),
            kept,
            kept + PIECES[1],
            PIECES[0] * (2 * (1 - z % 2) + which),
        )

    starts = (places_of(core), places_of(1 - core))

    lanes = (0, PIECES[0], PIECES[0] + PIECES[1], 2 * width - PIECES[3])
    tok_copies = [
        pltpu.make_async_copy(
            tokens_ref.at[:, pl.ds(pl.multiple_of(starts[0][j], 128), PIECES[j])],
            tok.at[:, pl.ds(lanes[j], PIECES[j])],
            in_sem.at[(0, 5, 6)[j]],
        )
        for j in range(3)
    ]
    wg_copy = pltpu.make_async_copy(w_gate_ref.at[0], wcat.at[:, pl.ds(0, BLK)], in_sem.at[1])
    wu_copy = pltpu.make_async_copy(w_up_ref.at[0], wcat.at[:, pl.ds(BLK, BLK)], in_sem.at[2])
    dh_copy = pltpu.make_async_copy(dh_ref, dh, in_sem.at[3])
    routes_copy = pltpu.make_async_copy(routes_ref, routes, in_sem.at[4])
    routes_copy.start()
    for copy in tok_copies:
        copy.start()
    dh_copy.start()
    wg_copy.start()
    wu_copy.start()

    barrier = pltpu.get_barrier_semaphore()

    def greet(e, d):
        pl.semaphore_signal(
            barrier, inc=1, device_id={"expert": e, "etp": d}, device_id_type=MESH
        )

    for o in range(1, EXPERTS):
        greet(peer(o), p)
    for o in range(EXPERTS):
        greet(peer(o), y_mate)
    greet(expert, core_mate)
    for dz in (1, ZS - 1):
        greet(expert, (p + 4 * dz) % (4 * ZS))

    lane = lax.broadcasted_iota(jnp.int32, (128, 128), 1)
    row = lax.broadcasted_iota(jnp.int32, (128, 128), 0)
    routes_copy.wait()
    names_0 = jnp.where(row == routes[0:1, :], 1.0, 0.0)
    names_1 = jnp.where(row == routes[1:2, :], 1.0, 0.0)
    names = names_0 + names_1
    before = jnp.where(row < lane, 1.0, 0.0).astype(BF16)
    position = dot(names.astype(BF16), before)
    position = jnp.where(names > 0.5, position, -1.0)
    slot = row[:CAP].astype(F32)
    places = []
    for e in range(EXPERTS):
        place = jnp.where(slot == position[e : e + 1, :], 1.0, 0.0)
        pmat[e] = place
        places.append(place)
    sends = []
    stores = []

    def finish():
        for copy in sends:
            copy.wait_send()
        for copy in stores:
            copy.wait()

    def remote(src, dst, send_sem, recv_sem, e, d):
        copy = pltpu.make_async_remote_copy(
            src_ref=src,
            dst_ref=dst,
            send_sem=send_sem,
            recv_sem=recv_sem,
            device_id={"expert": e, "etp": d},
            device_id_type=MESH,
        )
        copy.start()
        sends.append(copy)
        return copy

    def tell(step):
        for dz in (1 << step, ZS - (1 << step)):
            pl.semaphore_signal(
                known.at[step],
                inc=1,
                device_id={"expert": expert, "etp": (p + 4 * dz) % (4 * ZS)},
                device_id_type=MESH,
            )

    def hear(step):
        pl.semaphore_wait(known.at[step], 2)

    stage1 = {}
    by_slot = jnp.concatenate(places, axis=0).astype(BF16)
    for j in range(3):
        tok_copies[j].wait()
        placed = dot(by_slot, tok[:, lanes[j] : lanes[j] + PIECES[j]])
        mid = PIECES[j] // 2
        for e in range(EXPERTS):
            rows = placed[CAP * e : CAP * e + CAP]
            rows = jnp.concatenate([rows[:, :mid], rows[:, mid:]], axis=0)
            rows_out[j][e] = rows.astype(BF16)
        if j == 0:
            pl.semaphore_wait(barrier, (EXPERTS - 1) + EXPERTS + 1 + 2)
        for o in range(1, EXPERTS):
            stage1[j, o] = remote(
                rows_out[j].at[peer(o)],
                land[j].at[0, o],
                s1_send.at[j, o],
                s1_recv.at[j, o],
                peer(o),
                near(peer(o)),
            )
    tell(0)
    first = [places[e] * names_0[e : e + 1, :] for e in range(EXPERTS)]
    second = [places[e] * names_1[e : e + 1, :] for e in range(EXPERTS)]
    token_of = lax.broadcasted_iota(jnp.int32, (128, 256), 0)
    choice = lax.broadcasted_iota(jnp.int32, (128, 256), 1)
    even = jnp.where(choice == 2 * token_of, 1.0, 0.0).astype(BF16)
    odd = jnp.where(choice == 2 * token_of + 1, 1.0, 0.0).astype(BF16)
    placing = dot(jnp.concatenate(first, axis=0).astype(BF16), even)
    placing = placing + dot(jnp.concatenate(second, axis=0).astype(BF16), odd)
    dh_copy.wait()
    cot = dot(placing.astype(BF16), dh[...])
    for e in range(EXPERTS):
        padded = jnp.concatenate(
            [cot[CAP * e : CAP * e + CAP], jnp.zeros((8, 128), F32)], axis=0
        )
        cot_out[e] = padded.astype(BF16)
    cots = {}
    for o in FAR_FIRST:
        cots[o] = remote(
            cot_out.at[peer(o)], cot_land.at[o], cot_send.at[o], cot_recv.at[o], peer(o), p
        )
    for j in range(3):
        land[j][0, 0] = rows_out[j][expert]
    cot_land[0] = cot_out[expert]
    gather = jnp.concatenate(
        [pmat[peer(o)] for o in range(EXPERTS) for _ in range(2)], axis=0
    ).T.astype(BF16)

    def compact(r, j):
        mid = PIECES[j] // 2
        lane_at = lanes[j] % width
        for i in range(EXPERTS // 2):
            one = land[j][r, 2 * i].astype(F32)
            two = land[j][r, 2 * i + 1].astype(F32)
            left = jnp.concatenate([one[:CAP], two[:CAP]], axis=0)
            right = jnp.concatenate([one[CAP:], two[CAP:]], axis=0)
            at = pl.ds(2 * CAP * i, 2 * CAP)
            srows[2 * r + j // 2, at, pl.ds(lane_at, mid)] = left.astype(BF16)
            srows[2 * r + j // 2, at, pl.ds(lane_at + mid, mid)] = right.astype(BF16)

    def forward(r, j):
        compact(r, j)
        at = pl.multiple_of(starts[r][j], 128)
        rows = srows[2 * r + j // 2, :, pl.ds(lanes[j] % width, PIECES[j])]
        return dot(rows, wcat[pl.ds(at, PIECES[j]), :])

    def sort_weights(out_ref, which):
        for side in range(2):
            for i, dz in enumerate(ORDER):
                at = ((z + dz) % ZS) * 192 + side * 96 + which * OWNED
                out_ref[side, pl.ds(OWNED * i, OWNED), :] = wcat[
                    pl.ds(pl.multiple_of(at, 16), OWNED), :
                ]

    wg_copy.wait()
    wu_copy.wait()
    sort_weights(w_out, 1 - core)
    w_swap = remote(w_out, w_in, swap_send.at[0], swap_recv.at[0], expert, core_mate)
    sort_weights(w_own, core)
    hear(0)
    tell(1)

    passed = []

    def pass_on(j):
        passed.append(
            remote(
                land[j].at[0], land[j].at[1], c0_send.at[j], c0_recv.at[j], expert, core_mate
            )
        )

    def arrived(j):
        for o in range(1, EXPERTS):
            stage1[j, o].wait_recv()

    arrived(0)
    along = remote(land[0].at[0], land[3].at[0], z_send.at[0], z_recv.at[0], expert, z_to)
    pass_on(0)
    acts = forward(0, 0)
    hear(1)
    tell(2)
    arrived(1)
    pass_on(1)
    along.wait_recv()
    pass_on(3)
    acts = acts + forward(0, 1)
    acts = acts + forward(0, 3)
    passed[0].wait_recv()
    acts = acts + forward(1, 0)
    arrived(2)
    pass_on(2)
    acts = acts + forward(0, 2)
    for o in FAR_FIRST:
        cots[o].wait_recv()
    cotangent = jnp.concatenate(
        [cot_land[o].astype(F32)[:CAP] for o in range(EXPERTS)], axis=0
    )
    for copy, j in zip(passed[1:], (1, 3, 2)):
        copy.wait_recv()
        acts = acts + forward(1, j)

    gate_act, up_act = acts[:, :BLK], acts[:, BLK:]
    sig = jax.nn.sigmoid(gate_act)
    d_up = cotangent * gate_act * sig
    d_gate = cotangent * up_act * sig * (1.0 + gate_act * (1.0 - sig))
    d_both = jnp.concatenate([d_gate, d_up], axis=1)
    d_rows = d_both.astype(BF16)
    d_out[...] = d_rows
    d_swap = remote(d_out, d_in, swap_send.at[1], swap_recv.at[1], expert, core_mate)
    d_both = jnp.concatenate([d_both, jnp.zeros((384 - SLOTS, 2 * BLK), F32)], axis=0)
    d_t = d_both.T.astype(BF16)[:, :SLOTS]

    def grad_piece(r):
        grad = dot(d_t, srows[r])
        hi = grad.astype(BF16)
        lo = (grad - hi.astype(F32)).astype(BF16)
        a_hi[r] = hi
        a_lo[r] = lo
        if r == 0:
            gram[0] = dot_nt(hi, hi)
            gram[1] = dot_nt(hi, lo)
        else:
            gram[0] = gram[0] + dot_nt(hi, hi)
            gram[1] = gram[1] + dot_nt(hi, lo)

    wide_row = lax.broadcasted_iota(jnp.int32, (256, 256), 0)
    wide_lane = lax.broadcasted_iota(jnp.int32, (256, 256), 1)
    state = {}

    def ns_start():
        cross = gram[1]
        g = gram[0] + cross + cross.T
        g = jnp.where((wide_row < BLK) == (wide_lane < BLK), g, 0.0)
        diagonal = jnp.where(wide_row == wide_lane, g, 0.0)
        sum_gate = jnp.sum(diagonal[:BLK], keepdims=True)
        sum_up = jnp.sum(diagonal[BLK:], keepdims=True)
        scale = jnp.where(
            wide_row < BLK, lax.rsqrt(sum_gate + 1e-06), lax.rsqrt(sum_up + 1e-06)
        )
        state["scale"] = scale
        state["g"] = g * scale * scale

    def polynomial(g):
        square = dot_exact(g, g)
        return jnp.where(wide_row == wide_lane, NS_FIRST, 0.0) + NS_SECOND * g + NS_THIRD * square

    def ns_one():
        g = state["g"]
        poly = polynomial(g)
        state["m"] = poly
        state["g"] = dot_exact(dot_exact(g, poly), poly)

    def ns_two():
        g = state["g"]
        poly = polynomial(g)
        both = dot_exact(jnp.concatenate([state["m"], g], axis=0), poly)
        state["m"] = both[:256]
        state["g"] = dot_exact(both[256:], poly)

    def ns_three():
        m = dot_exact(state["m"], polynomial(state["g"])) * state["scale"]
        hi = m.astype(BF16)
        mix[0] = hi
        mix[1] = (m - hi.astype(F32)).astype(BF16)

    def update_piece(r):
        hi = a_hi[r]
        update = dot(mix[0], hi) + dot(mix[1], hi) + dot(mix[0], a_lo[r])
        update = update.T.astype(BF16)
        low = 0
        for i, j in enumerate((2 * (r % 2), 2 * (r % 2) + 1)):
            at = pl.ds(pl.multiple_of(starts[r // 2][j], 128), PIECES[j])
            here = pl.ds(low, PIECES[j])
            for k, out_ref in enumerate((update_gate_ref, update_up_ref)):
                updates[k, r, here] = update[low : low + PIECES[j], BLK * k : BLK * k + BLK]
                copy = pltpu.make_async_copy(
                    updates.at[k, r, here], out_ref.at[0, at], out_sem.at[k, r, i]
                )
                copy.start()
                stores.append(copy)
            low += PIECES[j]

    tasks = [functools.partial(grad_piece, r) for r in range(4)]
    tasks += [ns_start, ns_one, ns_two, ns_three]
    tasks += [functools.partial(update_piece, r) for r in range(4)]

    def work(count):
        for _ in range(count):
            if tasks:
                tasks.pop(0)()

    cols = width // STAGES

    def back(rows, weights, st):
        at = pl.ds(cols * st, cols)
        return dot_nt(rows, jnp.concatenate([weights[0, at], weights[1, at]], axis=0))

    totals = [back(d_rows, w_own, st) for st in range(STAGES)]
    w_swap.wait_recv()
    d_swap.wait_recv()
    d_mate = d_in[...]

    returns = {}
    for st in range(STAGES):
        totals[st] = totals[st] + back(d_mate, w_in, st)
        out_ref, in_ref = sums_out.at[st], sums_in.at[st]
        for o in FAR_FIRST + (0,):
            low, high = CAP * o, CAP * o + CAP
            for side in range(2):
                block = [
                    totals[st][low:high, at : at + cols // 2]
                    for at in (cols * side, cols * side + cols // 2)
                ]
                out_ref[o, side] = jnp.concatenate(block, axis=0).astype(BF16)
            for dy in (1, 0):
                to_y = (y + dy) % 2
                if o == 0 and dy == 0:
                    in_ref[0, 0] = out_ref[0, y]
                    continue
                returns[st, o, dy] = remote(
                    out_ref.at[o, to_y],
                    in_ref.at[o, dy],
                    a2a_send.at[st, o, dy],
                    a2a_recv.at[st, o, dy],
                    back_peer(o),
                    z * 4 + to_y * 2 + core,
                )
    hear(2)
    copies = {}
    for st in range(STAGES):
        work(WORK[st])
        left, right = [], []
        for o in range(EXPERTS):
            for dy in range(2):
                if (st, o, dy) in returns:
                    returns[st, o, dy].wait_recv()
                block = sums_in[st, o, dy].astype(F32)
                left.append(block[:CAP])
                right.append(block[CAP:])
        got = [jnp.concatenate(left, axis=0), jnp.concatenate(right, axis=0)]
        part = dot(gather, jnp.concatenate(got, axis=1).astype(BF16)).T
        for i, dz in enumerate(ORDER):
            low = max(OWNED * i, cols * st)
            high = min(OWNED * i + OWNED, cols * st + cols)
            if low >= high:
                continue
            value = part[low - cols * st : high - cols * st]
            if dz == 0:
                mine = value
                continue
            zx_out[dz, pl.ds(low - OWNED * i, high - low)] = value.astype(BF16)
            if high < OWNED * i + OWNED:
                continue
            copies[dz] = remote(
                zx_out.at[dz],
                zx_in.at[dz],
                zx_send.at[dz],
                zx_recv.at[dz],
                expert,
                (p + 4 * dz) % (4 * ZS),
            )
    work(len(tasks))
    for dz, copy in copies.items():
        copy.wait_recv()
        mine = mine + zx_in[dz].astype(F32)
    d_tokens_ref[...] = mine.astype(BF16)
    finish()


def hand_on(parts, t_ref, a_ref, b_ref, t_out, a_out, b_out, t_held, held, in_sem, out_sem):
    rows = a_ref.shape[1] // parts
    moves = [(t_ref, t_held, t_out, in_sem.at[0, parts], out_sem.at[0, parts])]
    for i in range(parts):
        at = pl.ds(i * rows, rows)
        for k, (src, dst) in enumerate(((a_ref, a_out), (b_ref, b_out))):
            moves.append(
                (src.at[0, at], held.at[k, at], dst.at[0, at], in_sem.at[k, i], out_sem.at[k, i])
            )
    loads = [pltpu.make_async_copy(src, mid, sem) for src, mid, _, sem, _ in moves]
    stores = [pltpu.make_async_copy(mid, dst, sem) for _, mid, dst, _, sem in moves]
    for load in loads:
        load.start()
    for load, store in zip(loads, stores):
        load.wait()
        store.start()
    for store in stores:
        store.wait()


def body(tokens, routes, w_gate, w_up, d_hidden):
    count, model_width = tokens.shape
    units = w_gate.shape[2]
    width = model_width // 4
    half = width // 2
    cols = width // STAGES
    dma = pltpu.SemaphoreType.DMA
    scratch = [
        pltpu.VMEM((2, count), jnp.int32),
        pltpu.VMEM((count, 2 * width - PIECES[3]), BF16),
        pltpu.VMEM((2 * count, units), BF16),
        pltpu.VMEM((2, 4, width, units), BF16),
        pltpu.VMEM((model_width, 2 * units), BF16),
        *[pltpu.VMEM((EXPERTS, 2 * CAP, PIECES[j] // 2), BF16) for j in range(3)],
        *[pltpu.VMEM((2, EXPERTS, 2 * CAP, PIECES[j] // 2), BF16) for j in range(4)],
        pltpu.VMEM((EXPERTS, 48, units), BF16),
        pltpu.VMEM((EXPERTS, 48, units), BF16),
        pltpu.VMEM((4, SLOTS, width), BF16),
        pltpu.VMEM((4, 2 * units, width), BF16),
        pltpu.VMEM((4, 2 * units, width), BF16),
        pltpu.VMEM((2, 2 * units, 2 * units), F32),
        pltpu.VMEM((2, 2 * units, 2 * units), BF16),
        pltpu.VMEM((2, width, 2 * units), BF16),
        pltpu.VMEM((2, width, 2 * units), BF16),
        pltpu.VMEM((2, width, 2 * units), BF16),
        pltpu.VMEM((SLOTS, 2 * units), BF16),
        pltpu.VMEM((SLOTS, 2 * units), BF16),
        pltpu.VMEM((STAGES, EXPERTS, 2, 2 * CAP, cols // 2), BF16),
        pltpu.VMEM((STAGES, EXPERTS, 2, 2 * CAP, cols // 2), BF16),
        pltpu.VMEM((ZS, 48, count), BF16),
        pltpu.VMEM((ZS, 48, count), BF16),
        pltpu.VMEM((EXPERTS, CAP, count), F32),
        pltpu.SemaphoreType.REGULAR((3,)),
        dma((7,)),
        dma((2, 4, 2)),
    ]
    for shape in (
        (3, EXPERTS),
        (EXPERTS,),
        (1,),
        (4,),
        (2,),
        (STAGES, EXPERTS, 2),
        (ZS,),
    ):
        scratch += [dma(shape), dma(shape)]
    vmem = pl.BlockSpec(memory_space=pltpu.VMEM)
    anywhere = pl.BlockSpec(memory_space=pl.ANY)
    d_tokens, update_gate, update_up = pl.pallas_call(
        kernel,
        out_shape=(
            jax.ShapeDtypeStruct((48, count), BF16),
            jax.ShapeDtypeStruct(w_gate.shape, BF16),
            jax.ShapeDtypeStruct(w_up.shape, BF16),
        ),
        in_specs=[anywhere] * 5,
        out_specs=(vmem, anywhere, anywhere),
        scratch_shapes=scratch,
        compiler_params=pltpu.CompilerParams(
            collective_id=0, has_side_effects=True, vmem_limit_bytes=56 * 1024 * 1024
        ),
    )(tokens, routes.T, w_gate, w_up, d_hidden.reshape(2 * count, units))
    parts = 4
    d_tokens, update_gate, update_up = pl.pallas_call(
        functools.partial(hand_on, parts),
        out_shape=(
            jax.ShapeDtypeStruct((48, count), BF16),
            jax.ShapeDtypeStruct(w_gate.shape, BF16),
            jax.ShapeDtypeStruct(w_up.shape, BF16),
        ),
        in_specs=[anywhere] * 3,
        out_specs=(anywhere,) * 3,
        scratch_shapes=[
            pltpu.VMEM((48, count), BF16),
            pltpu.VMEM((2, model_width, units), BF16),
            dma((2, parts + 1)),
            dma((2, parts + 1)),
        ],
    )(d_tokens, update_gate, update_up)
    return d_tokens.T, update_gate, update_up


def solution(mesh):
    in_specs = (
        P("expert", None),
        P("expert", None),
        P("expert", None, "etp"),
        P("expert", None, "etp"),
        P("expert", None, "etp"),
    )
    out_specs = (P("expert", "etp"), P("expert", None, "etp"), P("expert", None, "etp"))
    return jax.shard_map(body, mesh=mesh, in_specs=in_specs, out_specs=out_specs, check_vma=False)
```
